32 devices in a mesh: src: 4 (over z), tgt: 8 (over y, x, core).
Axes of the slice: x: 2, y: 2, z: 4, core: 2. Of those that a mesh axis runs over, the one named last changes fastest.
Arguments:
- generator: int32 [64], replicated, may hold values from 1 to 8191, as said below
- shift: float32 [64], replicated, may hold values from 0 to 1
- targets: float32 [64, 8192], P(None, 'tgt'), may hold values from -8 to 8
- log_weights: float32 [8192], P('tgt'), may hold values from -20 to 150
Outputs:
- potential_f: float32 [8192], P('src')
- potential_g: float32 [8192], P('tgt')
The draws below stay inside these ranges and needn't reach their ends.
Inputs may be any that keep to these rules, and one draw needn't show every extreme that they name: `generator`: odd integers.
All inputs are finite; a program needn't handle non-finite values.
Results may differ from the reference program's by a relative error of at most 0.0003.
Values sent between devices are 32-bit elements; how exact they have to be, the bound alone decides.
A program may use at most 64 MiB of HBM per device.

```python
import math
import jax
import jax.numpy as jnp
from jax import lax

DIM = 64
ITERS = 2
NS = 8192
NT = 8192


def draw_generator(key, part):
    return 2 * jax.random.randint(key, (DIM,), 0, NS // 2, dtype=jnp.int32) + 1


def draw_targets(key, part):
    first = jax.random.fold_in(jax.random.fold_in(key, 11), 0)
    base = 0.6 * jax.random.normal(first, (DIM, NT), jnp.float32)
    return jnp.clip(base, -8.0, 8.0)


def draw_log_weights(key, part):
    rising = 1.1 * jnp.arange(NT, dtype=jnp.float32) / NT
    noise = 3.0 * jax.random.normal(jax.random.fold_in(key, 23), (NT,), jnp.float32)
    return jnp.clip(noise, -12.0, 12.0) + rising


def setup_inputs(seed: int = 0) -> dict:
    key_of = jax.random.split(jax.random.key(seed), 5)
    generator = draw_generator(jax.random.fold_in(key_of[4], 71), 0)
    shift = jnp.clip(jax.random.uniform(key_of[1], (DIM,), jnp.float32, 0.0, 1.0), 0.0, 1.0)
    targets = draw_targets(jax.random.fold_in(key_of[4], 71), 0)
    log_weights = draw_log_weights(jax.random.fold_in(key_of[4], 71), 0)
    return dict(generator=generator, shift=shift, targets=targets, log_weights=log_weights)


blur_level = 0.1
highest = lax.Precision.HIGHEST


def lattice_block(generator, shift, start, count, modulus):
    index = start + jnp.arange(count, dtype=jnp.int32)
    folded = (index[None, :] * generator[:, None]) % modulus
    phase = folded.astype(jnp.float32) / modulus + shift[:, None]
    return jnp.sin(2.0 * jnp.pi * phase)


def cost_block(points, targets):
    cross = lax.dot_general(points, targets, (((0,), (0,)), ((), ())), precision=highest, preferred_element_type=jnp.float32)
    near = 0.5 * jnp.sum(points * points, 0)
    far = 0.5 * jnp.sum(targets * targets, 0)
    return near[:, None] + far[None, :] - cross


def reference(generator, shift, targets, log_weights):
    peak = jnp.max(log_weights)
    log_b = log_weights - (peak + jnp.log(jnp.sum(jnp.exp(log_weights - peak))))
    log_a = -math.log(NS)
    block = min(512, NS)
    count = NS // block
    potential_g = jnp.zeros((NT,), jnp.float32)
    potential_f = jnp.zeros((NS,), jnp.float32)
    for step in range(ITERS):
        def row_pass(index, current_g=potential_g):
            points = lattice_block(generator, shift, index * block, block, NS)
            scores = log_b[None, :] + (current_g[None, :] - cost_block(points, targets)) / blur_level
            top = jnp.max(scores, 1)
            return -blur_level * (top + jnp.log(jnp.sum(jnp.exp(scores - top[:, None]), 1)))

        potential_f = lax.map(row_pass, jnp.arange(count, dtype=jnp.int32)).reshape(NS)

        def column_pass(carry, index, current_f=potential_f):
            peak_c, total_c = carry
            start = index * block
            points = lattice_block(generator, shift, start, block, NS)
            part = lax.dynamic_slice_in_dim(current_f, start, block)
            scores = log_a + (part[:, None] - cost_block(points, targets)) / blur_level
            top = jnp.maximum(peak_c, jnp.max(scores, 0))
            total = total_c * jnp.exp(peak_c - top) + jnp.sum(jnp.exp(scores - top[None, :]), 0)
            return (top, total), None

        start_carry = (jnp.full((NT,), -1e30, jnp.float32), jnp.zeros((NT,), jnp.float32))
        (top, total), unused = lax.scan(column_pass, start_carry, jnp.arange(count, dtype=jnp.int32))
        potential_g = -blur_level * (top + jnp.log(total))
    return potential_f, potential_g
```

```python
import functools
import math

import jax
import jax.numpy as jnp
from jax import lax
from jax.experimental import pallas as pl
from jax.experimental.pallas import tpu as pltpu
from jax.sharding import PartitionSpec as P

SRC_DEV = 2048
ITERS = 2
LANES = 128
WIDE = 256

blur_level = 0.1
log2_e = math.log2(math.e)
scale = log2_e / blur_level
MESH = pl.DeviceIdType.MESH
f32 = jnp.float32
bf16 = jnp.bfloat16


def sine_cosine(turns):
    half = (turns - jnp.round(turns)) * f32(math.pi)
    square = half * half
    sine = f32(1.0 / math.factorial(13))
    cosine = f32(1.0 / math.factorial(12))
    for order in (11, 9, 7, 5, 3, 1):
        sign = -1.0 if (order // 2) % 2 else 1.0
        sine = sine * square + f32(sign / math.factorial(order))
    for order in (10, 8, 6, 4, 2, 0):
        sign = -1.0 if (order // 2) % 2 else 1.0
        cosine = cosine * square + f32(sign / math.factorial(order))
    sine = sine * half
    return 2.0 * sine * cosine, 1.0 - 2.0 * sine * sine


def wrap(value, modulus):
    return value & (modulus - 1) if modulus & (modulus - 1) == 0 else lax.rem(value, modulus)


def log_sum(terms):
    top = functools.reduce(jnp.maximum, terms)
    total = functools.reduce(jnp.add, [jnp.exp2(term - top) for term in terms])
    return top + jnp.log(total) * f32(log2_e)


def chunk_lse(left, right):
    scores = lax.dot_general(
        left, right, (((1,), (1,)), ((), ())), preferred_element_type=f32
    )
    top = jnp.max(scores, 0, keepdims=True)
    total = jnp.sum(jnp.exp2(scores - top), 0, keepdims=True)
    return top + jnp.log(total) * f32(log2_e)


def place(values, static, left_ref):
    blocks = values.shape[0]
    high = values.astype(bf16).astype(f32)
    rest = values - high
    mid = rest.astype(bf16).astype(f32)
    low = rest - mid
    filler = [jnp.zeros((LANES // 2, LANES), f32), high, mid, low]
    spare = LANES // 2 - 3 * blocks
    if spare:
        filler.append(jnp.zeros((spare, LANES), f32))
    turned = jnp.concatenate(filler, 0).T
    lane = lax.broadcasted_iota(jnp.int32, (LANES, LANES), 1)
    for block in range(blocks):
        rows = pl.ds(block * LANES, LANES)
        kept = jnp.where(
            lane < LANES // 2,
            static[rows, LANES:].astype(f32),
            jnp.where(lax.rem(lane - LANES // 2, blocks) == block, turned, 0.0),
        )
        left_ref[rows, LANES:] = kept.astype(bf16)


def kernel(
    sizes, generator_ref, shift_ref, targets_ref, weights_ref, f_ref, g_ref,
    a_left, a_right, b_left, b_right, squares, pair, far_ref, near_ref,
    row_out, row_in, col_out, col_in, norm_out, norm_in,
    row_send, row_recv, col_send, col_recv, norm_send, norm_recv,
):
    src, tgt = sizes
    modulus = SRC_DEV * src
    my_src, my_tgt = lax.axis_index("src"), lax.axis_index("tgt")
    src_peers = [lax.rem(my_src + step, src) for step in range(1, src)]
    tgt_peers = [lax.rem(my_tgt + step, tgt) for step in range(1, tgt)]
    barrier = pltpu.get_barrier_semaphore()
    for peer in tgt_peers:
        pl.semaphore_signal(barrier, inc=1, device_id=(my_src, peer), device_id_type=MESH)
    for peer in src_peers:
        pl.semaphore_signal(barrier, inc=1, device_id=(peer, my_tgt), device_id_type=MESH)

    def row_copy(step, number):
        return pltpu.make_async_remote_copy(
            src_ref=row_out.at[step], dst_ref=row_in.at[step, number],
            send_sem=row_send.at[step, number], recv_sem=row_recv.at[step, number],
            device_id=(my_src, tgt_peers[number]), device_id_type=MESH,
        )

    def col_copy(step, number):
        return pltpu.make_async_remote_copy(
            src_ref=col_out.at[step], dst_ref=col_in.at[step, number],
            send_sem=col_send.at[step, number], recv_sem=col_recv.at[step, number],
            device_id=(src_peers[number], my_tgt), device_id_type=MESH,
        )

    def norm_copy(number):
        return pltpu.make_async_remote_copy(
            src_ref=norm_out, dst_ref=norm_in.at[number],
            send_sem=norm_send.at[number], recv_sem=norm_recv.at[number],
            device_id=(my_src, tgt_peers[number]), device_id_type=MESH,
        )

    blocks_i = SRC_DEV // LANES
    columns = targets_ref.shape[1]
    blocks_j = columns // LANES
    lane = lax.broadcasted_iota(jnp.int32, (LANES, LANES), 1)
    first = lane < LANES // 2

    pair[0:1, : LANES // 2] = generator_ref[...].astype(f32)
    pair[1:2, : LANES // 2] = shift_ref[...]
    both = pair[0:2, :]
    low_half = lax.broadcasted_iota(jnp.int32, (2, LANES), 1) < LANES // 2
    both = jnp.where(low_half, both, pltpu.roll(both, LANES // 2, 1))
    generator = both[0:1, :].astype(jnp.int32)
    shift = both[1:2, :]
    inner = lax.broadcasted_iota(jnp.int32, (LANES, LANES), 0)
    sin_in, cos_in = sine_cosine(
        wrap(inner * generator, modulus).astype(f32) / modulus
    )
    outer = lax.broadcasted_iota(jnp.int32, (blocks_i, LANES), 0) * LANES + my_src * SRC_DEV
    sin_out, cos_out = sine_cosine(
        wrap(outer * generator, modulus).astype(f32) / modulus + shift
    )
    for block in range(blocks_i):
        rows = pl.ds(block * LANES, LANES)
        points = (
            sin_out[block : block + 1, :] * cos_in + cos_out[block : block + 1, :] * sin_in
        )
        high = points.astype(bf16)
        a_left[rows, :LANES] = high
        a_right[rows, :LANES] = high
        a_right[rows, LANES:] = jnp.where(first, points - high.astype(f32), 1.0).astype(bf16)
        square = points * points
        square_high = square.astype(bf16).astype(f32)
        squares[rows, :] = jnp.where(first, square_high, square - square_high).astype(bf16)

    for block in range(blocks_j):
        rows = pl.ds(block * LANES, LANES)
        part = targets_ref[:, block * LANES : (block + 1) * LANES]
        far_ref[block : block + 1, :] = 0.5 * jnp.sum(part * part, 0, keepdims=True)
        part = part * f32(scale)
        high = part.astype(bf16).astype(f32)
        turned = jnp.concatenate([high, part - high], 0).T
        b_left[rows, :LANES] = turned.astype(bf16)
        b_right[rows, :LANES] = turned.astype(bf16)
        b_right[rows, LANES:] = jnp.where(first, turned, 1.0).astype(bf16)

    weights = weights_ref[...] * f32(log2_e)
    far = far_ref[...] * f32(scale)
    log_count = f32(math.log2(modulus))
    potential_g = -far
    for step in range(ITERS):
        place(weights + potential_g, b_right, b_left)
        for chunk in range(SRC_DEV // WIDE):
            part = chunk_lse(b_left[...], a_right[pl.ds(chunk * WIDE, WIDE), :])
            for piece in range(WIDE // LANES):
                at = chunk * (WIDE // LANES) + piece
                row_out[step, at : at + 1, :] = part[:, piece * LANES : (piece + 1) * LANES]
        if step == 0:
            peak = jnp.max(weights, keepdims=True)
            total = jnp.sum(jnp.exp2(weights - peak), keepdims=True)
            norm_out[...] = jnp.broadcast_to(
                peak + jnp.log(total) * f32(log2_e), (8, LANES)
            )
            pl.semaphore_wait(barrier, src - 1 + tgt - 1)
        for number in range(tgt - 1):
            row_copy(step, number).start()
        if step == 0:
            for number in range(tgt - 1):
                norm_copy(number).start()
            sums = lax.dot_general(
                jnp.ones((8, LANES), bf16), squares[...],
                (((1,), (1,)), ((), ())), preferred_element_type=f32,
            )
            for block in range(blocks_i):
                near_ref[block : block + 1, :] = (
                    0.5 * sums[0:1, block * LANES : (block + 1) * LANES]
                )
        for number in range(tgt - 1):
            row_copy(step, number).wait_recv()
        potential_f = -log_sum(
            [row_out[step]] + [row_in[step, number] for number in range(tgt - 1)]
        )
        place(potential_f, a_right, a_left)
        for chunk in range(columns // WIDE):
            part = chunk_lse(a_left[...], b_right[pl.ds(chunk * WIDE, WIDE), :])
            for piece in range(WIDE // LANES):
                at = chunk * (WIDE // LANES) + piece
                col_out[step, at : at + 1, :] = part[:, piece * LANES : (piece + 1) * LANES]
        for number in range(src - 1):
            col_copy(step, number).start()
        if step == 0:
            for number in range(tgt - 1):
                norm_copy(number).wait_recv()
            norm = log_sum(
                [norm_out[...]] + [norm_in[number] for number in range(tgt - 1)]
            )[0:1, :]
        if step == ITERS - 1:
            f_ref[...] = (potential_f + norm) * f32(1.0 / scale) + near_ref[...]
        for number in range(src - 1):
            col_copy(step, number).wait_recv()
        sums = log_sum([col_out[step]] + [col_in[step, number] for number in range(src - 1)])
        potential_g = log_count - sums - norm
    g_ref[...] = potential_g * f32(1.0 / scale) + far_ref[...]
    for step in range(ITERS):
        for number in range(tgt - 1):
            row_copy(step, number).wait_send()
        for number in range(src - 1):
            col_copy(step, number).wait_send()
    for number in range(tgt - 1):
        norm_copy(number).wait_send()


def local(sizes, generator, shift, targets, log_weights):
    src, tgt = sizes
    columns = targets.shape[1]
    blocks_i, blocks_j = SRC_DEV // LANES, columns // LANES
    vmem = pl.BlockSpec(memory_space=pltpu.VMEM)
    dma = pltpu.SemaphoreType.DMA
    potential_f, potential_g = pl.pallas_call(
        functools.partial(kernel, sizes),
        out_shape=(
            jax.ShapeDtypeStruct((blocks_i, LANES), f32),
            jax.ShapeDtypeStruct((blocks_j, LANES), f32),
        ),
        in_specs=[vmem] * 4,
        out_specs=(vmem, vmem),
        scratch_shapes=[
            pltpu.VMEM((SRC_DEV, 2 * LANES), bf16),
            pltpu.VMEM((SRC_DEV, 2 * LANES), bf16),
            pltpu.VMEM((columns, 2 * LANES), bf16),
            pltpu.VMEM((columns, 2 * LANES), bf16),
            pltpu.VMEM((SRC_DEV, LANES), bf16),
            pltpu.VMEM((8, LANES), f32),
            pltpu.VMEM((blocks_j, LANES), f32),
            pltpu.VMEM((blocks_i, LANES), f32),
            pltpu.VMEM((ITERS, blocks_i, LANES), f32),
            pltpu.VMEM((ITERS, tgt - 1, blocks_i, LANES), f32),
            pltpu.VMEM((ITERS, blocks_j, LANES), f32),
            pltpu.VMEM((ITERS, src - 1, blocks_j, LANES), f32),
            pltpu.VMEM((8, LANES), f32),
            pltpu.VMEM((tgt - 1, 8, LANES), f32),
            dma((ITERS, tgt - 1)),
            dma((ITERS, tgt - 1)),
            dma((ITERS, src - 1)),
            dma((ITERS, src - 1)),
            dma((tgt - 1,)),
            dma((tgt - 1,)),
        ],
        compiler_params=pltpu.CompilerParams(
            collective_id=0, has_side_effects=True, vmem_limit_bytes=40 * 2**20
        ),
    )(
        generator.reshape(1, -1),
        shift.reshape(1, -1),
        targets,
        log_weights.reshape(blocks_j, LANES),
    )
    return potential_f.reshape(-1), potential_g.reshape(-1)


def solution(mesh):
    sizes = (mesh.shape["src"], mesh.shape["tgt"])
    in_specs = (P(), P(), P(None, "tgt"), P("tgt"))
    out_specs = (P("src"), P("tgt"))
    return jax.shard_map(
        functools.partial(local, sizes), mesh=mesh,
        in_specs=in_specs, out_specs=out_specs, check_vma=False,
    )
```

```python
import functools
import math

import jax
import jax.numpy as jnp
from jax import lax
from jax.experimental import pallas as pl
from jax.experimental.pallas import tpu as pltpu
from jax.sharding import PartitionSpec as P

SRC_DEV = 2048
ITERS = 2
LANES = 128
WIDE = 256
GROUP = 8

blur_level = 0.1
log2_e = math.log2(math.e)
scale = log2_e / blur_level
MESH = pl.DeviceIdType.MESH
f32 = jnp.float32
bf16 = jnp.bfloat16


def sine_cosine(turns):
    half = (turns - jnp.round(turns)) * f32(math.pi)
    square = half * half
    sine = f32(1.0 / math.factorial(13))
    cosine = f32(1.0 / math.factorial(12))
    for order in (11, 9, 7, 5, 3, 1):
        sign = -1.0 if (order // 2) % 2 else 1.0
        sine = sine * square + f32(sign / math.factorial(order))
    for order in (10, 8, 6, 4, 2, 0):
        sign = -1.0 if (order // 2) % 2 else 1.0
        cosine = cosine * square + f32(sign / math.factorial(order))
    sine = sine * half
    return 2.0 * sine * cosine, 1.0 - 2.0 * sine * sine


def wrap(value, modulus):
    return value & (modulus - 1) if modulus & (modulus - 1) == 0 else lax.rem(value, modulus)


def log_sum(terms):
    top = functools.reduce(jnp.maximum, terms)
    total = functools.reduce(jnp.add, [jnp.exp2(term - top) for term in terms])
    return top + jnp.log(total) * f32(log2_e)


def fold(combine, scores):
    parts = scores.reshape(-1, 8 * GROUP, scores.shape[1])
    return combine(combine(parts, 0), 0, keepdims=True)


def sweep(left_ref, right_ref, count, tops, totals):
    def product(chunk):
        return lax.dot_general(
            left_ref[...], right_ref[pl.ds(chunk * WIDE, WIDE), :],
            (((1,), (1,)), ((), ())), preferred_element_type=f32,
        )

    scores = product(0)
    for chunk in range(count):
        later = product(chunk + 1) if chunk + 1 < count else None
        top = fold(jnp.max, scores)
        total = fold(jnp.sum, jnp.exp2(scores - top))
        for piece in range(WIDE // LANES):
            at = chunk * (WIDE // LANES) + piece
            cut = slice(piece * LANES, (piece + 1) * LANES)
            tops[at : at + 1, :] = top[:, cut]
            totals[at : at + 1, :] = total[:, cut]
        scores = later


def place(values, static, left_ref):
    blocks = values.shape[0]
    high = values.astype(bf16).astype(f32)
    rest = values - high
    mid = rest.astype(bf16).astype(f32)
    low = rest - mid
    filler = [jnp.zeros((LANES // 2, LANES), f32), high, mid, low]
    spare = LANES // 2 - 3 * blocks
    if spare:
        filler.append(jnp.zeros((spare, LANES), f32))
    turned = jnp.concatenate(filler, 0).T
    lane = lax.broadcasted_iota(jnp.int32, (LANES, LANES), 1)
    for block in range(blocks):
        rows = pl.ds(block * LANES, LANES)
        kept = jnp.where(
            lane < LANES // 2,
            static[rows, LANES:].astype(f32),
            jnp.where(lax.rem(lane - LANES // 2, blocks) == block, turned, 0.0),
        )
        left_ref[rows, LANES:] = kept.astype(bf16)


def kernel(
    sizes, generator_hbm, shift_hbm, targets_hbm, weights_hbm, f_ref, g_ref,
    generator_ref, shift_ref, targets_ref, weights_ref,
    a_left, a_right, b_left, b_right, squares, pair, far_ref, near_ref,
    row_tops, row_totals, col_tops, col_totals,
    row_out, row_in, col_out, col_in, norm_out, norm_in,
    row_send, row_recv, col_send, col_recv, norm_send, norm_recv, load,
):
    src, tgt = sizes
    modulus = SRC_DEV * src
    my_src, my_tgt = lax.axis_index("src"), lax.axis_index("tgt")
    src_peers = [lax.rem(my_src + step, src) for step in range(1, src)]
    tgt_peers = [lax.rem(my_tgt + step, tgt) for step in range(1, tgt)]
    loads = [
        pltpu.make_async_copy(source, place_in, load.at[number])
        for number, (source, place_in) in enumerate((
            (generator_hbm, generator_ref), (shift_hbm, shift_ref),
            (targets_hbm, targets_ref), (weights_hbm, weights_ref),
        ))
    ]
    for copy in loads:
        copy.start()
    barrier = pltpu.get_barrier_semaphore()
    for peer in tgt_peers:
        pl.semaphore_signal(barrier, inc=1, device_id=(my_src, peer), device_id_type=MESH)
    for peer in src_peers:
        pl.semaphore_signal(barrier, inc=1, device_id=(peer, my_tgt), device_id_type=MESH)

    def row_copy(step, number):
        return pltpu.make_async_remote_copy(
            src_ref=row_out.at[step], dst_ref=row_in.at[step, number],
            send_sem=row_send.at[step, number], recv_sem=row_recv.at[step, number],
            device_id=(my_src, tgt_peers[number]), device_id_type=MESH,
        )

    def col_copy(step, number):
        return pltpu.make_async_remote_copy(
            src_ref=col_out.at[step], dst_ref=col_in.at[step, number],
            send_sem=col_send.at[step, number], recv_sem=col_recv.at[step, number],
            device_id=(src_peers[number], my_tgt), device_id_type=MESH,
        )

    def norm_copy(number):
        return pltpu.make_async_remote_copy(
            src_ref=norm_out, dst_ref=norm_in.at[number],
            send_sem=norm_send.at[number], recv_sem=norm_recv.at[number],
            device_id=(my_src, tgt_peers[number]), device_id_type=MESH,
        )

    blocks_i = SRC_DEV // LANES
    columns = targets_ref.shape[1]
    blocks_j = columns // LANES
    lane = lax.broadcasted_iota(jnp.int32, (LANES, LANES), 1)
    first = lane < LANES // 2

    loads[0].wait()
    loads[1].wait()
    pair[0:1, : LANES // 2] = generator_ref[...].astype(f32)
    pair[1:2, : LANES // 2] = shift_ref[...]
    both = pair[0:2, :]
    low_half = lax.broadcasted_iota(jnp.int32, (2, LANES), 1) < LANES // 2
    both = jnp.where(low_half, both, pltpu.roll(both, LANES // 2, 1))
    generator = both[0:1, :].astype(jnp.int32)
    shift = both[1:2, :]
    inner = lax.broadcasted_iota(jnp.int32, (LANES, LANES), 0)
    sin_in, cos_in = sine_cosine(
        wrap(inner * generator, modulus).astype(f32) / modulus
    )
    outer = lax.broadcasted_iota(jnp.int32, (blocks_i, LANES), 0) * LANES + my_src * SRC_DEV
    sin_out, cos_out = sine_cosine(
        wrap(outer * generator, modulus).astype(f32) / modulus + shift
    )
    for block in range(blocks_i):
        rows = pl.ds(block * LANES, LANES)
        points = (
            sin_out[block : block + 1, :] * cos_in + cos_out[block : block + 1, :] * sin_in
        )
        high = points.astype(bf16)
        a_left[rows, :LANES] = high
        a_right[rows, :LANES] = high
        a_right[rows, LANES:] = jnp.where(first, points - high.astype(f32), 1.0).astype(bf16)
        square = points * points
        square_high = square.astype(bf16).astype(f32)
        squares[rows, :] = jnp.where(first, square_high, square - square_high).astype(bf16)

    loads[2].wait()
    loads[3].wait()
    for block in range(blocks_j):
        rows = pl.ds(block * LANES, LANES)
        part = targets_ref[:, block * LANES : (block + 1) * LANES]
        far_ref[block : block + 1, :] = 0.5 * jnp.sum(part * part, 0, keepdims=True)
        part = part * f32(scale)
        high = part.astype(bf16).astype(f32)
        turned = jnp.concatenate([high, part - high], 0).T
        b_left[rows, :LANES] = turned.astype(bf16)
        b_right[rows, :LANES] = turned.astype(bf16)
        b_right[rows, LANES:] = jnp.where(first, turned, 1.0).astype(bf16)

    weights = weights_ref[...] * f32(log2_e)
    far = far_ref[...] * f32(scale)
    log_count = f32(math.log2(modulus))
    potential_g = -far
    for step in range(ITERS):
        place(weights + potential_g, b_right, b_left)
        sweep(b_left, a_right, SRC_DEV // WIDE, row_tops, row_totals)
        row_out[step] = row_tops[...] + jnp.log(row_totals[...]) * f32(log2_e)
        if step == 0:
            peak = jnp.max(weights, keepdims=True)
            total = jnp.sum(jnp.exp2(weights - peak), keepdims=True)
            norm_out[...] = jnp.broadcast_to(
                peak + jnp.log(total) * f32(log2_e), (8, LANES)
            )
            pl.semaphore_wait(barrier, src - 1 + tgt - 1)
        for number in range(tgt - 1):
            row_copy(step, number).start()
        if step == 0:
            for number in range(tgt - 1):
                norm_copy(number).start()
            sums = lax.dot_general(
                jnp.ones((8, LANES), bf16), squares[...],
                (((1,), (1,)), ((), ())), preferred_element_type=f32,
            )
            for block in range(blocks_i):
                near_ref[block : block + 1, :] = (
                    0.5 * sums[0:1, block * LANES : (block + 1) * LANES]
                )
        for number in range(tgt - 1):
            row_copy(step, number).wait_recv()
        potential_f = -log_sum(
            [row_out[step]] + [row_in[step, number] for number in range(tgt - 1)]
        )
        place(potential_f, a_right, a_left)
        sweep(a_left, b_right, columns // WIDE, col_tops, col_totals)
        col_out[step] = col_tops[...] + jnp.log(col_totals[...]) * f32(log2_e)
        for number in range(src - 1):
            col_copy(step, number).start()
        if step == 0:
            for number in range(tgt - 1):
                norm_copy(number).wait_recv()
            norm = log_sum(
                [norm_out[...]] + [norm_in[number] for number in range(tgt - 1)]
            )[0:1, :]
        if step == ITERS - 1:
            f_ref[...] = (potential_f + norm) * f32(1.0 / scale) + near_ref[...]
        for number in range(src - 1):
            col_copy(step, number).wait_recv()
        sums = log_sum([col_out[step]] + [col_in[step, number] for number in range(src - 1)])
        potential_g = log_count - sums - norm
    g_ref[...] = potential_g * f32(1.0 / scale) + far_ref[...]
    for step in range(ITERS):
        for number in range(tgt - 1):
            row_copy(step, number).wait_send()
        for number in range(src - 1):
            col_copy(step, number).wait_send()
    for number in range(tgt - 1):
        norm_copy(number).wait_send()


def local(sizes, generator, shift, targets, log_weights):
    src, tgt = sizes
    columns = targets.shape[1]
    blocks_i, blocks_j = SRC_DEV // LANES, columns // LANES
    vmem = pl.BlockSpec(memory_space=pltpu.VMEM)
    dma = pltpu.SemaphoreType.DMA
    potential_f, potential_g = pl.pallas_call(
        functools.partial(kernel, sizes),
        out_shape=(
            jax.ShapeDtypeStruct((blocks_i, LANES), f32),
            jax.ShapeDtypeStruct((blocks_j, LANES), f32),
        ),
        in_specs=[pl.BlockSpec(memory_space=pltpu.HBM)] * 4,
        out_specs=(vmem, vmem),
        scratch_shapes=[
            pltpu.VMEM((1, generator.shape[0]), jnp.int32),
            pltpu.VMEM((1, shift.shape[0]), f32),
            pltpu.VMEM(targets.shape, f32),
            pltpu.VMEM((blocks_j, LANES), f32),
            pltpu.VMEM((SRC_DEV, 2 * LANES), bf16),
            pltpu.VMEM((SRC_DEV, 2 * LANES), bf16),
            pltpu.VMEM((columns, 2 * LANES), bf16),
            pltpu.VMEM((columns, 2 * LANES), bf16),
            pltpu.VMEM((SRC_DEV, LANES), bf16),
            pltpu.VMEM((8, LANES), f32),
            pltpu.VMEM((blocks_j, LANES), f32),
            pltpu.VMEM((blocks_i, LANES), f32),
            pltpu.VMEM((blocks_i, LANES), f32),
            pltpu.VMEM((blocks_i, LANES), f32),
            pltpu.VMEM((blocks_j, LANES), f32),
            pltpu.VMEM((blocks_j, LANES), f32),
            pltpu.VMEM((ITERS, blocks_i, LANES), f32),
            pltpu.VMEM((ITERS, tgt - 1, blocks_i, LANES), f32),
            pltpu.VMEM((ITERS, blocks_j, LANES), f32),
            pltpu.VMEM((ITERS, src - 1, blocks_j, LANES), f32),
            pltpu.VMEM((8, LANES), f32),
            pltpu.VMEM((tgt - 1, 8, LANES), f32),
            dma((ITERS, tgt - 1)),
            dma((ITERS, tgt - 1)),
            dma((ITERS, src - 1)),
            dma((ITERS, src - 1)),
            dma((tgt - 1,)),
            dma((tgt - 1,)),
            dma((4,)),
        ],
        compiler_params=pltpu.CompilerParams(
            collective_id=0, has_side_effects=True, vmem_limit_bytes=64 * 2**20 - 2**17
        ),
    )(
        generator.reshape(1, -1),
        shift.reshape(1, -1),
        targets,
        log_weights.reshape(blocks_j, LANES),
    )
    return potential_f.reshape(-1), potential_g.reshape(-1)


def solution(mesh):
    sizes = (mesh.shape["src"], mesh.shape["tgt"])
    in_specs = (P(), P(), P(None, "tgt"), P("tgt"))
    out_specs = (P("src"), P("tgt"))
    return jax.shard_map(
        functools.partial(local, sizes), mesh=mesh,
        in_specs=in_specs, out_specs=out_specs, check_vma=False,
    )
```

```python
import functools
import math

import jax
import jax.numpy as jnp
from jax import lax
from jax.experimental import pallas as pl
from jax.experimental.pallas import tpu as pltpu
from jax.sharding import PartitionSpec as P

SRC_DEV = 2048
ITERS = 2
LANES = 128
WIDE = 256
TILE = 64
LIMIT = 40 * 2**20
PRODUCT = 1024

blur_level = 0.1
log2_e = math.log2(math.e)
scale = log2_e / blur_level
MESH = pl.DeviceIdType.MESH
f32 = jnp.float32
bf16 = jnp.bfloat16


def sine_cosine(turns):
    half = (turns - jnp.round(turns)) * f32(math.pi)
    square = half * half
    sine = f32(1.0 / math.factorial(13))
    cosine = f32(1.0 / math.factorial(12))
    for order in (11, 9, 7, 5, 3, 1):
        sign = -1.0 if (order // 2) % 2 else 1.0
        sine = sine * square + f32(sign / math.factorial(order))
    for order in (10, 8, 6, 4, 2, 0):
        sign = -1.0 if (order // 2) % 2 else 1.0
        cosine = cosine * square + f32(sign / math.factorial(order))
    sine = sine * half
    return 2.0 * sine * cosine, 1.0 - 2.0 * sine * sine


def wrap(value, modulus):
    return value & (modulus - 1) if modulus & (modulus - 1) == 0 else lax.rem(value, modulus)


def log_sum(terms):
    top = functools.reduce(jnp.maximum, terms)
    total = functools.reduce(jnp.add, [jnp.exp2(term - top) for term in terms])
    return top + jnp.log(total) * f32(log2_e)


def fold(combine, scores, rows):
    running = None
    for start in range(0, rows, TILE):
        running = combine(running, scores[pl.ds(start, TILE), :])
    return running


def sweep(left_ref, right_ref, buffers, tops, totals):
    rows, count = left_ref.shape[0], right_ref.shape[1] // WIDE

    def product(chunk):
        right = right_ref[:, pl.ds(chunk * WIDE, WIDE)]
        for start in range(0, rows, PRODUCT):
            part = pl.ds(start, PRODUCT)
            buffers[chunk % 2][part, :] = jnp.dot(
                left_ref[part, :], right, preferred_element_type=f32
            )

    product(0)
    for chunk in range(count):
        if chunk + 1 < count:
            product(chunk + 1)
        scores = buffers[chunk % 2]
        top = fold(lambda a, b: b if a is None else jnp.maximum(a, b), scores, rows)
        top = jnp.max(top, 0, keepdims=True)
        shift = jnp.broadcast_to(top, (TILE, WIDE))

        def add(total, part):
            part = jnp.exp2(part - shift)
            return part if total is None else total + part

        total = jnp.sum(fold(add, scores, rows), 0, keepdims=True)
        for piece in range(WIDE // LANES):
            at = chunk * (WIDE // LANES) + piece
            cut = slice(piece * LANES, (piece + 1) * LANES)
            tops[at : at + 1, :] = top[:, cut]
            totals[at : at + 1, :] = total[:, cut]


def place(values, static, left_ref):
    blocks = values.shape[0]
    high = values.astype(bf16).astype(f32)
    rest = values - high
    mid = rest.astype(bf16).astype(f32)
    low = rest - mid
    filler = [jnp.zeros((LANES // 2, LANES), f32), high, mid, low]
    spare = LANES // 2 - 3 * blocks
    if spare:
        filler.append(jnp.zeros((spare, LANES), f32))
    turned = jnp.concatenate(filler, 0).T
    lane = lax.broadcasted_iota(jnp.int32, (LANES, LANES), 1)
    owner = jnp.where(lane < LANES // 2, -1, wrap(lane, blocks))
    for block in range(blocks):
        rows = pl.ds(block * LANES, LANES)
        added = jnp.where(owner == block, turned, 0.0).astype(bf16)
        left_ref[rows, LANES:] = static[rows, :] + added


def kernel(
    sizes, generator_hbm, shift_hbm, targets_hbm, weights_hbm, out_ref,
    generator_ref, shift_ref, targets_ref, weights_ref,
    a_left, a_right, a_static, b_left, b_right, b_static, buffer_0, buffer_1, pair, far_ref, near_ref,
    row_tops, row_totals, col_tops, col_totals,
    row_out, row_in, col_out, col_in, norm_out, norm_in,
    row_send, row_recv, col_send, col_recv, norm_send, norm_recv, load,
):
    src, tgt = sizes
    modulus = SRC_DEV * src
    my_src, my_tgt = lax.axis_index("src"), lax.axis_index("tgt")
    src_peers = [lax.rem(my_src + step, src) for step in range(1, src)]
    tgt_peers = [lax.rem(my_tgt + step, tgt) for step in range(1, tgt)]
    loads = [
        pltpu.make_async_copy(source, place_in, load.at[number])
        for number, (source, place_in) in enumerate((
            (generator_hbm, generator_ref), (shift_hbm, shift_ref),
            (targets_hbm, targets_ref), (weights_hbm, weights_ref),
        ))
    ]
    for copy in loads:
        copy.start()
    barrier = pltpu.get_barrier_semaphore()
    for peer in tgt_peers:
        pl.semaphore_signal(barrier, inc=1, device_id=(my_src, peer), device_id_type=MESH)
    for peer in src_peers:
        pl.semaphore_signal(barrier, inc=1, device_id=(peer, my_tgt), device_id_type=MESH)

    def row_copy(step, number):
        return pltpu.make_async_remote_copy(
            src_ref=row_out.at[step], dst_ref=row_in.at[step, number],
            send_sem=row_send.at[step, number], recv_sem=row_recv.at[step, number],
            device_id=(my_src, tgt_peers[number]), device_id_type=MESH,
        )

    def col_copy(step, number):
        return pltpu.make_async_remote_copy(
            src_ref=col_out.at[step], dst_ref=col_in.at[step, number],
            send_sem=col_send.at[step, number], recv_sem=col_recv.at[step, number],
            device_id=(src_peers[number], my_tgt), device_id_type=MESH,
        )

    def norm_copy(number):
        return pltpu.make_async_remote_copy(
            src_ref=norm_out, dst_ref=norm_in.at[number],
            send_sem=norm_send.at[number], recv_sem=norm_recv.at[number],
            device_id=(my_src, tgt_peers[number]), device_id_type=MESH,
        )

    blocks_i = SRC_DEV // LANES
    columns = targets_ref.shape[1]
    blocks_j = columns // LANES
    lane = lax.broadcasted_iota(jnp.int32, (LANES, LANES), 1)
    first = lane < LANES // 2

    loads[0].wait()
    loads[1].wait()
    pair[0:1, : LANES // 2] = generator_ref[...].astype(f32)
    pair[1:2, : LANES // 2] = shift_ref[...]
    both = pair[0:2, :]
    low_half = lax.broadcasted_iota(jnp.int32, (2, LANES), 1) < LANES // 2
    both = jnp.where(low_half, both, pltpu.roll(both, LANES // 2, 1))
    generator = both[0:1, :].astype(jnp.int32)
    shift = both[1:2, :]
    inner = lax.broadcasted_iota(jnp.int32, (LANES, LANES), 0)
    sin_in, cos_in = sine_cosine(
        wrap(inner * generator, modulus).astype(f32) / modulus
    )
    outer = lax.broadcasted_iota(jnp.int32, (blocks_i, LANES), 0) * LANES + my_src * SRC_DEV
    sin_out, cos_out = sine_cosine(
        wrap(outer * generator, modulus).astype(f32) / modulus + shift
    )
    half = LANES // 2
    for block in range(blocks_i):
        rows = pl.ds(block * LANES, LANES)
        points = (
            sin_out[block : block + 1, :] * cos_in + cos_out[block : block + 1, :] * sin_in
        )
        high = points.astype(bf16)
        a_left[rows, :LANES] = high
        a_static[rows, :] = jnp.where(first, points - high.astype(f32), 0.0).astype(bf16)
    sin_in, cos_in = sin_in.T[:half, :], cos_in.T[:half, :]
    outside = jnp.concatenate(
        [sin_out, cos_out, jnp.zeros((LANES - 2 * blocks_i, LANES), f32)], 0
    ).T[:half, :]
    for block in range(blocks_i):
        cut = pl.ds(block * LANES, LANES)
        points = (
            outside[:, block : block + 1] * cos_in
            + outside[:, blocks_i + block : blocks_i + block + 1] * sin_in
        )
        near_ref[block : block + 1, :] = 0.5 * jnp.sum(points * points, 0, keepdims=True)
        high = points.astype(bf16)
        a_right[:half, cut] = high
        a_right[half : 2 * half, cut] = high
        a_right[2 * half : 3 * half, cut] = (points - high.astype(f32)).astype(bf16)
    a_right[3 * half :, :] = jnp.ones((half, SRC_DEV), bf16)

    loads[2].wait()
    loads[3].wait()
    for block in range(blocks_j):
        rows = pl.ds(block * LANES, LANES)
        part = targets_ref[:, block * LANES : (block + 1) * LANES]
        far_ref[block : block + 1, :] = 0.5 * jnp.sum(part * part, 0, keepdims=True)
        part = part * f32(scale)
        high = part.astype(bf16)
        low = part - high.astype(f32)
        turned = jnp.concatenate([high.astype(f32), low], 0).T
        b_left[rows, :LANES] = turned.astype(bf16)
        b_static[rows, :] = jnp.where(first, turned, 0.0).astype(bf16)
        b_right[:half, rows] = high
        b_right[half : 2 * half, rows] = low.astype(bf16)
        b_right[2 * half : 3 * half, rows] = high
    b_right[3 * half :, :] = jnp.ones((half, columns), bf16)

    weights = weights_ref[...] * f32(log2_e)
    far = far_ref[...] * f32(scale)
    log_count = f32(math.log2(modulus))
    potential_g = -far
    buffers = (buffer_0, buffer_1)
    for step in range(ITERS):
        place(weights + potential_g, b_static, b_left)
        sweep(b_left, a_right, buffers, row_tops, row_totals)
        row_out[step] = row_tops[...] + jnp.log(row_totals[...]) * f32(log2_e)
        if step == 0:
            peak = jnp.max(weights, keepdims=True)
            total = jnp.sum(jnp.exp2(weights - peak), keepdims=True)
            norm_out[...] = jnp.broadcast_to(
                peak + jnp.log(total) * f32(log2_e), (8, LANES)
            )
            pl.semaphore_wait(barrier, src - 1 + tgt - 1)
        for number in range(tgt - 1):
            row_copy(step, number).start()
        if step == 0:
            for number in range(tgt - 1):
                norm_copy(number).start()
        for number in range(tgt - 1):
            row_copy(step, number).wait_recv()
        potential_f = -log_sum(
            [row_out[step]] + [row_in[step, number] for number in range(tgt - 1)]
        )
        place(potential_f, a_static, a_left)
        sweep(a_left, b_right, buffers, col_tops, col_totals)
        col_out[step] = col_tops[...] + jnp.log(col_totals[...]) * f32(log2_e)
        for number in range(src - 1):
            col_copy(step, number).start()
        if step == 0:
            for number in range(tgt - 1):
                norm_copy(number).wait_recv()
            norm = log_sum(
                [norm_out[...]] + [norm_in[number] for number in range(tgt - 1)]
            )[0:1, :]
        if step == ITERS - 1:
            out_ref[:blocks_i, :] = (potential_f + norm) * f32(1.0 / scale) + near_ref[...]
        for number in range(src - 1):
            col_copy(step, number).wait_recv()
        sums = log_sum([col_out[step]] + [col_in[step, number] for number in range(src - 1)])
        potential_g = log_count - sums - norm
    out_ref[blocks_i:, :] = potential_g * f32(1.0 / scale) + far_ref[...]
    for step in range(ITERS):
        for number in range(tgt - 1):
            row_copy(step, number).wait_send()
        for number in range(src - 1):
            col_copy(step, number).wait_send()
    for number in range(tgt - 1):
        norm_copy(number).wait_send()


def local(sizes, generator, shift, targets, log_weights):
    src, tgt = sizes
    columns = targets.shape[1]
    blocks_i, blocks_j = SRC_DEV // LANES, columns // LANES
    vmem = pl.BlockSpec(memory_space=pltpu.VMEM)
    dma = pltpu.SemaphoreType.DMA
    both = pl.pallas_call(
        functools.partial(kernel, sizes),
        out_shape=jax.ShapeDtypeStruct((blocks_i + blocks_j, LANES), f32),
        in_specs=[pl.BlockSpec(memory_space=pltpu.HBM)] * 4,
        out_specs=vmem,
        scratch_shapes=[
            pltpu.VMEM((1, generator.shape[0]), jnp.int32),
            pltpu.VMEM((1, shift.shape[0]), f32),
            pltpu.VMEM(targets.shape, f32),
            pltpu.VMEM((blocks_j, LANES), f32),
            pltpu.VMEM((SRC_DEV, 2 * LANES), bf16),
            pltpu.VMEM((2 * LANES, SRC_DEV), bf16),
            pltpu.VMEM((SRC_DEV, LANES), bf16),
            pltpu.VMEM((columns, 2 * LANES), bf16),
            pltpu.VMEM((2 * LANES, columns), bf16),
            pltpu.VMEM((columns, LANES), bf16),
            pltpu.VMEM((max(SRC_DEV, columns), WIDE), f32),
            pltpu.VMEM((max(SRC_DEV, columns), WIDE), f32),
            pltpu.VMEM((8, LANES), f32),
            pltpu.VMEM((blocks_j, LANES), f32),
            pltpu.VMEM((blocks_i, LANES), f32),
            pltpu.VMEM((blocks_i, LANES), f32),
            pltpu.VMEM((blocks_i, LANES), f32),
            pltpu.VMEM((blocks_j, LANES), f32),
            pltpu.VMEM((blocks_j, LANES), f32),
            pltpu.VMEM((ITERS, blocks_i, LANES), f32),
            pltpu.VMEM((ITERS, tgt - 1, blocks_i, LANES), f32),
            pltpu.VMEM((ITERS, blocks_j, LANES), f32),
            pltpu.VMEM((ITERS, src - 1, blocks_j, LANES), f32),
            pltpu.VMEM((8, LANES), f32),
            pltpu.VMEM((tgt - 1, 8, LANES), f32),
            dma((ITERS, tgt - 1)),
            dma((ITERS, tgt - 1)),
            dma((ITERS, src - 1)),
            dma((ITERS, src - 1)),
            dma((tgt - 1,)),
            dma((tgt - 1,)),
            dma((4,)),
        ],
        compiler_params=pltpu.CompilerParams(
            collective_id=0, has_side_effects=True, vmem_limit_bytes=LIMIT
        ),
    )(
        generator.reshape(1, -1),
        shift.reshape(1, -1),
        targets,
        log_weights.reshape(blocks_j, LANES),
    )
    return both[:blocks_i].reshape(-1), both[blocks_i:].reshape(-1)


def solution(mesh):
    sizes = (mesh.shape["src"], mesh.shape["tgt"])
    in_specs = (P(), P(), P(None, "tgt"), P("tgt"))
    out_specs = (P("src"), P("tgt"))
    return jax.shard_map(
        functools.partial(local, sizes), mesh=mesh,
        in_specs=in_specs, out_specs=out_specs, check_vma=False,
    )
```

```python
import functools
import math

import jax
import jax.numpy as jnp
from jax import lax
from jax.experimental import pallas as pl
from jax.experimental.pallas import tpu as pltpu
from jax.sharding import PartitionSpec as P

SRC_DEV = 2048
ITERS = 2
LANES = 128
WIDE = 256
TILE = 64
LIMIT = 40 * 2**20
HALVES = 2

blur_level = 0.1
log2_e = math.log2(math.e)
scale = log2_e / blur_level
MESH = pl.DeviceIdType.MESH
f32 = jnp.float32
bf16 = jnp.bfloat16


def sine_cosine(turns):
    half = (turns - jnp.round(turns)) * f32(math.pi)
    square = half * half
    sine = f32(1.0 / math.factorial(13))
    cosine = f32(1.0 / math.factorial(12))
    for order in (11, 9, 7, 5, 3, 1):
        sign = -1.0 if (order // 2) % 2 else 1.0
        sine = sine * square + f32(sign / math.factorial(order))
    for order in (10, 8, 6, 4, 2, 0):
        sign = -1.0 if (order // 2) % 2 else 1.0
        cosine = cosine * square + f32(sign / math.factorial(order))
    sine = sine * half
    return 2.0 * sine * cosine, 1.0 - 2.0 * sine * sine


def wrap(value, modulus):
    return value & (modulus - 1) if modulus & (modulus - 1) == 0 else lax.rem(value, modulus)


def log_sum(terms):
    top = functools.reduce(jnp.maximum, terms)
    total = functools.reduce(jnp.add, [jnp.exp2(term - top) for term in terms])
    return top + jnp.log(total) * f32(log2_e)


def fold(combine, scores, rows):
    running = None
    for start in range(0, rows, TILE):
        running = combine(running, scores[pl.ds(start, TILE), :])
    return running


def sweep(left_ref, right_ref, buffers, rows, tops, totals, after=None):
    first, size = rows
    count = right_ref.shape[1] // WIDE

    def product(chunk):
        right = right_ref[:, pl.ds(chunk * WIDE, WIDE)]
        buffers[chunk % 2][pl.ds(0, size), :] = jnp.dot(
            left_ref[pl.ds(first, size), :], right, preferred_element_type=f32
        )

    product(0)
    for chunk in range(count):
        if chunk + 1 < count:
            product(chunk + 1)
        scores = buffers[chunk % 2]
        top = fold(lambda a, b: b if a is None else jnp.maximum(a, b), scores, size)
        top = jnp.max(top, 0, keepdims=True)
        shift = jnp.broadcast_to(top, (TILE, WIDE))

        def add(total, part):
            part = jnp.exp2(part - shift)
            return part if total is None else total + part

        total = jnp.sum(fold(add, scores, size), 0, keepdims=True)
        for piece in range(WIDE // LANES):
            at = chunk * (WIDE // LANES) + piece
            cut = slice(piece * LANES, (piece + 1) * LANES)
            tops[at : at + 1, :] = top[:, cut]
            totals[at : at + 1, :] = total[:, cut]
        if after is not None:
            after(chunk)


def place(values, static, left_ref, first=0):
    blocks = values.shape[0]
    high = values.astype(bf16).astype(f32)
    rest = values - high
    mid = rest.astype(bf16).astype(f32)
    low = rest - mid
    filler = [jnp.zeros((LANES // 2, LANES), f32), high, mid, low]
    spare = LANES // 2 - 3 * blocks
    if spare:
        filler.append(jnp.zeros((spare, LANES), f32))
    turned = jnp.concatenate(filler, 0).T
    lane = lax.broadcasted_iota(jnp.int32, (LANES, LANES), 1)
    owner = jnp.where(lane < LANES // 2, -1, wrap(lane, blocks))
    for block in range(blocks):
        rows = pl.ds(first + block * LANES, LANES)
        added = jnp.where(owner == block, turned, 0.0).astype(bf16)
        left_ref[rows, LANES:] = static[rows, :] + added


def kernel(
    sizes, generator_hbm, shift_hbm, targets_hbm, weights_hbm, out_ref,
    generator_ref, shift_ref, targets_ref, weights_ref,
    a_left, a_right, a_static, b_left, b_right, b_static, buffer_0, buffer_1, pair, far_ref, near_ref,
    row_tops, row_totals, col_tops, col_totals,
    row_out, row_in, col_out, col_in, norm_out, norm_in,
    row_send, row_recv, col_send, col_recv, norm_send, norm_recv, load,
):
    src, tgt = sizes
    modulus = SRC_DEV * src
    my_src, my_tgt = lax.axis_index("src"), lax.axis_index("tgt")
    src_peers = [lax.rem(my_src + step, src) for step in range(1, src)]
    tgt_peers = [lax.rem(my_tgt + step, tgt) for step in range(1, tgt)]
    loads = [
        pltpu.make_async_copy(source, place_in, load.at[number])
        for number, (source, place_in) in enumerate((
            (generator_hbm, generator_ref), (shift_hbm, shift_ref),
            (targets_hbm, targets_ref), (weights_hbm, weights_ref),
        ))
    ]
    for copy in loads:
        copy.start()
    barrier = pltpu.get_barrier_semaphore()
    for peer in tgt_peers:
        pl.semaphore_signal(barrier, inc=1, device_id=(my_src, peer), device_id_type=MESH)
    for peer in src_peers:
        pl.semaphore_signal(barrier, inc=1, device_id=(peer, my_tgt), device_id_type=MESH)

    def row_copy(step, half, number):
        return pltpu.make_async_remote_copy(
            src_ref=row_out.at[step, half], dst_ref=row_in.at[step, half, number],
            send_sem=row_send.at[step, half, number],
            recv_sem=row_recv.at[step, half, number],
            device_id=(my_src, tgt_peers[number]), device_id_type=MESH,
        )

    def col_copy(step, number):
        return pltpu.make_async_remote_copy(
            src_ref=col_out.at[step], dst_ref=col_in.at[step, number],
            send_sem=col_send.at[step, number], recv_sem=col_recv.at[step, number],
            device_id=(src_peers[number], my_tgt), device_id_type=MESH,
        )

    def norm_copy(number):
        return pltpu.make_async_remote_copy(
            src_ref=norm_out, dst_ref=norm_in.at[number],
            send_sem=norm_send.at[number], recv_sem=norm_recv.at[number],
            device_id=(my_src, tgt_peers[number]), device_id_type=MESH,
        )

    blocks_i = SRC_DEV // LANES
    columns = targets_ref.shape[1]
    blocks_j = columns // LANES
    lane = lax.broadcasted_iota(jnp.int32, (LANES, LANES), 1)
    first = lane < LANES // 2

    loads[0].wait()
    loads[1].wait()
    pair[0:1, : LANES // 2] = generator_ref[...].astype(f32)
    pair[1:2, : LANES // 2] = shift_ref[...]
    both = pair[0:2, :]
    low_half = lax.broadcasted_iota(jnp.int32, (2, LANES), 1) < LANES // 2
    both = jnp.where(low_half, both, pltpu.roll(both, LANES // 2, 1))
    generator = both[0:1, :].astype(jnp.int32)
    shift = both[1:2, :]
    inner = lax.broadcasted_iota(jnp.int32, (LANES, LANES), 0)
    sin_in, cos_in = sine_cosine(
        wrap(inner * generator, modulus).astype(f32) / modulus
    )
    outer = lax.broadcasted_iota(jnp.int32, (blocks_i, LANES), 0) * LANES + my_src * SRC_DEV
    sin_out, cos_out = sine_cosine(
        wrap(outer * generator, modulus).astype(f32) / modulus + shift
    )
    half = LANES // 2
    for block in range(blocks_i):
        rows = pl.ds(block * LANES, LANES)
        points = (
            sin_out[block : block + 1, :] * cos_in + cos_out[block : block + 1, :] * sin_in
        )
        high = points.astype(bf16)
        a_left[rows, :LANES] = high
        a_static[rows, :] = jnp.where(first, points - high.astype(f32), 0.0).astype(bf16)
    sin_in, cos_in = sin_in.T[:half, :], cos_in.T[:half, :]
    outside = jnp.concatenate(
        [sin_out, cos_out, jnp.zeros((LANES - 2 * blocks_i, LANES), f32)], 0
    ).T[:half, :]
    for block in range(blocks_i):
        cut = pl.ds(block * LANES, LANES)
        points = (
            outside[:, block : block + 1] * cos_in
            + outside[:, blocks_i + block : blocks_i + block + 1] * sin_in
        )
        near_ref[block : block + 1, :] = 0.5 * jnp.sum(points * points, 0, keepdims=True)
        high = points.astype(bf16)
        a_right[:half, cut] = high
        a_right[half : 2 * half, cut] = high
        a_right[2 * half : 3 * half, cut] = (points - high.astype(f32)).astype(bf16)
    a_right[3 * half :, :] = jnp.ones((half, SRC_DEV), bf16)

    loads[2].wait()
    loads[3].wait()
    for block in range(blocks_j):
        rows = pl.ds(block * LANES, LANES)
        part = targets_ref[:, block * LANES : (block + 1) * LANES]
        far_ref[block : block + 1, :] = 0.5 * jnp.sum(part * part, 0, keepdims=True)
        part = part * f32(scale)
        high = part.astype(bf16)
        low = part - high.astype(f32)
        turned = jnp.concatenate([high.astype(f32), low], 0).T
        b_left[rows, :LANES] = turned.astype(bf16)
        b_static[rows, :] = jnp.where(first, turned, 0.0).astype(bf16)
        b_right[:half, rows] = high
        b_right[half : 2 * half, rows] = low.astype(bf16)
        b_right[2 * half : 3 * half, rows] = high
    b_right[3 * half :, :] = jnp.ones((half, columns), bf16)

    weights = weights_ref[...] * f32(log2_e)
    far = far_ref[...] * f32(scale)
    log_count = f32(math.log2(modulus))
    potential_g = -far
    buffers = (buffer_0, buffer_1)
    share = blocks_i // HALVES
    for step in range(ITERS):
        place(weights + potential_g, b_static, b_left)

        def send(chunk, step=step):
            half, rest = divmod((chunk + 1) * WIDE, share * LANES)
            if rest:
                return
            half = half - 1
            cut = pl.ds(half * share, share)
            row_out[step, half] = row_tops[cut, :] + jnp.log(row_totals[cut, :]) * f32(log2_e)
            if step == 0 and half == 0:
                pl.semaphore_wait(barrier, src - 1 + tgt - 1)
            for number in range(tgt - 1):
                row_copy(step, half, number).start()

        sweep(b_left, a_right, buffers, (0, columns), row_tops, row_totals, send)
        if step == 0:
            peak = jnp.max(weights, keepdims=True)
            total = jnp.sum(jnp.exp2(weights - peak), keepdims=True)
            norm_out[...] = jnp.broadcast_to(
                peak + jnp.log(total) * f32(log2_e), (8, LANES)
            )
            for number in range(tgt - 1):
                norm_copy(number).start()
        parts, potential_f = [], []
        for half in range(HALVES):
            for number in range(tgt - 1):
                row_copy(step, half, number).wait_recv()
            potential_f.append(-log_sum(
                [row_out[step, half]]
                + [row_in[step, half, number] for number in range(tgt - 1)]
            ))
            rows = (half * share * LANES, share * LANES)
            place(potential_f[half], a_static, a_left, rows[0])
            sweep(a_left, b_right, buffers, rows, col_tops, col_totals)
            parts.append(col_tops[...] + jnp.log(col_totals[...]) * f32(log2_e))
        col_out[step] = log_sum(parts)
        for number in range(src - 1):
            col_copy(step, number).start()
        if step == 0:
            for number in range(tgt - 1):
                norm_copy(number).wait_recv()
            norm = log_sum(
                [norm_out[...]] + [norm_in[number] for number in range(tgt - 1)]
            )[0:1, :]
        if step == ITERS - 1:
            for half in range(HALVES):
                cut = pl.ds(half * share, share)
                out_ref[cut, :] = (
                    (potential_f[half] + norm) * f32(1.0 / scale) + near_ref[cut, :]
                )
        for number in range(src - 1):
            col_copy(step, number).wait_recv()
        sums = log_sum([col_out[step]] + [col_in[step, number] for number in range(src - 1)])
        potential_g = log_count - sums - norm
    out_ref[blocks_i:, :] = potential_g * f32(1.0 / scale) + far_ref[...]
    for step in range(ITERS):
        for half in range(HALVES):
            for number in range(tgt - 1):
                row_copy(step, half, number).wait_send()
        for number in range(src - 1):
            col_copy(step, number).wait_send()
    for number in range(tgt - 1):
        norm_copy(number).wait_send()


def local(sizes, generator, shift, targets, log_weights):
    src, tgt = sizes
    columns = targets.shape[1]
    blocks_i, blocks_j = SRC_DEV // LANES, columns // LANES
    vmem = pl.BlockSpec(memory_space=pltpu.VMEM)
    dma = pltpu.SemaphoreType.DMA
    both = pl.pallas_call(
        functools.partial(kernel, sizes),
        out_shape=jax.ShapeDtypeStruct((blocks_i + blocks_j, LANES), f32),
        in_specs=[pl.BlockSpec(memory_space=pltpu.HBM)] * 4,
        out_specs=vmem,
        scratch_shapes=[
            pltpu.VMEM((1, generator.shape[0]), jnp.int32),
            pltpu.VMEM((1, shift.shape[0]), f32),
            pltpu.VMEM(targets.shape, f32),
            pltpu.VMEM((blocks_j, LANES), f32),
            pltpu.VMEM((SRC_DEV, 2 * LANES), bf16),
            pltpu.VMEM((2 * LANES, SRC_DEV), bf16),
            pltpu.VMEM((SRC_DEV, LANES), bf16),
            pltpu.VMEM((columns, 2 * LANES), bf16),
            pltpu.VMEM((2 * LANES, columns), bf16),
            pltpu.VMEM((columns, LANES), bf16),
            pltpu.VMEM((max(SRC_DEV, columns), WIDE), f32),
            pltpu.VMEM((max(SRC_DEV, columns), WIDE), f32),
            pltpu.VMEM((8, LANES), f32),
            pltpu.VMEM((blocks_j, LANES), f32),
            pltpu.VMEM((blocks_i, LANES), f32),
            pltpu.VMEM((blocks_i, LANES), f32),
            pltpu.VMEM((blocks_i, LANES), f32),
            pltpu.VMEM((blocks_j, LANES), f32),
            pltpu.VMEM((blocks_j, LANES), f32),
            pltpu.VMEM((ITERS, HALVES, blocks_i // HALVES, LANES), f32),
            pltpu.VMEM((ITERS, HALVES, tgt - 1, blocks_i // HALVES, LANES), f32),
            pltpu.VMEM((ITERS, blocks_j, LANES), f32),
            pltpu.VMEM((ITERS, src - 1, blocks_j, LANES), f32),
            pltpu.VMEM((8, LANES), f32),
            pltpu.VMEM((tgt - 1, 8, LANES), f32),
            dma((ITERS, HALVES, tgt - 1)),
            dma((ITERS, HALVES, tgt - 1)),
            dma((ITERS, src - 1)),
            dma((ITERS, src - 1)),
            dma((tgt - 1,)),
            dma((tgt - 1,)),
            dma((4,)),
        ],
        compiler_params=pltpu.CompilerParams(
            collective_id=0, has_side_effects=True, vmem_limit_bytes=LIMIT
        ),
    )(
        generator.reshape(1, -1),
        shift.reshape(1, -1),
        targets,
        log_weights.reshape(blocks_j, LANES),
    )
    return both[:blocks_i].reshape(-1), both[blocks_i:].reshape(-1)


def solution(mesh):
    sizes = (mesh.shape["src"], mesh.shape["tgt"])
    in_specs = (P(), P(), P(None, "tgt"), P("tgt"))
    out_specs = (P("src"), P("tgt"))
    return jax.shard_map(
        functools.partial(local, sizes), mesh=mesh,
        in_specs=in_specs, out_specs=out_specs, check_vma=False,
    )
```

```python
import functools
import math

import jax
import jax.numpy as jnp
from jax import lax
from jax.experimental import pallas as pl
from jax.experimental.pallas import tpu as pltpu
from jax.sharding import PartitionSpec as P

SRC_DEV = 2048
ITERS = 2
LANES = 128
WIDE = 256
TILE = 64
LIMIT = 40 * 2**20
HALVES = 2

blur_level = 0.1
log2_e = math.log2(math.e)
scale = log2_e / blur_level
MESH = pl.DeviceIdType.MESH
f32 = jnp.float32
bf16 = jnp.bfloat16


def sine_cosine(turns):
    half = (turns - jnp.round(turns)) * f32(math.pi)
    square = half * half
    sine = f32(1.0 / math.factorial(13))
    cosine = f32(1.0 / math.factorial(12))
    for order in (11, 9, 7, 5, 3, 1):
        sign = -1.0 if (order // 2) % 2 else 1.0
        sine = sine * square + f32(sign / math.factorial(order))
    for order in (10, 8, 6, 4, 2, 0):
        sign = -1.0 if (order // 2) % 2 else 1.0
        cosine = cosine * square + f32(sign / math.factorial(order))
    sine = sine * half
    return 2.0 * sine * cosine, 1.0 - 2.0 * sine * sine


def wrap(value, modulus):
    return value & (modulus - 1) if modulus & (modulus - 1) == 0 else lax.rem(value, modulus)


def log_sum(terms):
    top = functools.reduce(jnp.maximum, terms)
    total = functools.reduce(jnp.add, [jnp.exp2(term - top) for term in terms])
    return top + jnp.log(total) * f32(log2_e)


def fold(combine, scores, rows):
    running = None
    for start in range(0, rows, TILE):
        running = combine(running, scores[pl.ds(start, TILE), :])
    return running


def sweep(left_ref, right_ref, buffers, rows, tops, totals, after=None):
    first, size = rows
    count = right_ref.shape[1] // WIDE

    def product(chunk):
        scores = jnp.dot(
            left_ref[pl.ds(first, size), :],
            right_ref[:, pl.ds(chunk * WIDE, WIDE)],
            preferred_element_type=f32,
        )
        buffers[chunk % 2][pl.ds(0, size), :] = scores
        running = scores[:TILE]
        for start in range(TILE, size, TILE):
            running = jnp.maximum(running, scores[start : start + TILE])
        return jnp.max(running, 0, keepdims=True)

    later = product(0)
    for chunk in range(count):
        top = later
        if chunk + 1 < count:
            later = product(chunk + 1)
        scores = buffers[chunk % 2]
        shift = jnp.broadcast_to(top, (TILE, WIDE))

        def add(total, part):
            part = jnp.exp2(part - shift)
            return part if total is None else total + part

        total = jnp.sum(fold(add, scores, size), 0, keepdims=True)
        for piece in range(WIDE // LANES):
            at = chunk * (WIDE // LANES) + piece
            cut = slice(piece * LANES, (piece + 1) * LANES)
            tops[at : at + 1, :] = top[:, cut]
            totals[at : at + 1, :] = total[:, cut]
        if after is not None:
            after(chunk)


def place(values, static, left_ref, first=0):
    blocks = values.shape[0]
    high = values.astype(bf16).astype(f32)
    rest = values - high
    mid = rest.astype(bf16).astype(f32)
    low = rest - mid
    filler = [jnp.zeros((LANES // 2, LANES), f32), high, mid, low]
    spare = LANES // 2 - 3 * blocks
    if spare:
        filler.append(jnp.zeros((spare, LANES), f32))
    turned = jnp.concatenate(filler, 0).T.astype(bf16)
    lane = lax.broadcasted_iota(jnp.int32, (16, LANES), 1)
    owner = jnp.where(lane < LANES // 2, -1, wrap(lane, blocks))
    for block in range(blocks):
        rows = pl.ds(first + block * LANES, LANES)
        chosen = jnp.where(owner == block, 1.0, 0.0).astype(bf16)
        chosen = jnp.concatenate([chosen] * (LANES // 16), 0)
        left_ref[rows, LANES:] = static[rows, :] + turned * chosen


def kernel(
    sizes, generator_ref, shift_ref, targets_ref, weights_ref, out_ref,
    a_left, a_right, a_static, b_left, b_right, b_static, buffer_0, buffer_1, pair, far_ref, near_ref,
    row_tops, row_totals, col_tops, col_totals,
    row_out, row_in, col_out, col_in, norm_out, norm_in,
    row_send, row_recv, col_send, col_recv, norm_send, norm_recv,
):
    src, tgt = sizes
    modulus = SRC_DEV * src
    my_src, my_tgt = lax.axis_index("src"), lax.axis_index("tgt")
    src_peers = [lax.rem(my_src + step, src) for step in range(1, src)]
    tgt_peers = [lax.rem(my_tgt + step, tgt) for step in range(1, tgt)]
    barrier = pltpu.get_barrier_semaphore()
    for peer in tgt_peers:
        pl.semaphore_signal(barrier, inc=1, device_id=(my_src, peer), device_id_type=MESH)
    for peer in src_peers:
        pl.semaphore_signal(barrier, inc=1, device_id=(peer, my_tgt), device_id_type=MESH)

    def row_copy(step, half, number):
        return pltpu.make_async_remote_copy(
            src_ref=row_out.at[step, half], dst_ref=row_in.at[step, half, number],
            send_sem=row_send.at[step, half, number],
            recv_sem=row_recv.at[step, half, number],
            device_id=(my_src, tgt_peers[number]), device_id_type=MESH,
        )

    def col_copy(step, number):
        return pltpu.make_async_remote_copy(
            src_ref=col_out.at[step], dst_ref=col_in.at[step, number],
            send_sem=col_send.at[step, number], recv_sem=col_recv.at[step, number],
            device_id=(src_peers[number], my_tgt), device_id_type=MESH,
        )

    def norm_copy(number):
        return pltpu.make_async_remote_copy(
            src_ref=norm_out, dst_ref=norm_in.at[number],
            send_sem=norm_send.at[number], recv_sem=norm_recv.at[number],
            device_id=(my_src, tgt_peers[number]), device_id_type=MESH,
        )

    blocks_i = SRC_DEV // LANES
    columns = targets_ref.shape[1]
    blocks_j = columns // LANES
    lane = lax.broadcasted_iota(jnp.int32, (LANES, LANES), 1)
    first = lane < LANES // 2

    pair[0:1, : LANES // 2] = generator_ref[...].astype(f32)
    pair[1:2, : LANES // 2] = shift_ref[...]
    both = pair[0:2, :]
    low_half = lax.broadcasted_iota(jnp.int32, (2, LANES), 1) < LANES // 2
    both = jnp.where(low_half, both, pltpu.roll(both, LANES // 2, 1))
    generator = both[0:1, :].astype(jnp.int32)
    shift = both[1:2, :]
    inner = lax.broadcasted_iota(jnp.int32, (LANES, LANES), 0)
    sin_in, cos_in = sine_cosine(
        wrap(inner * generator, modulus).astype(f32) / modulus
    )
    outer = lax.broadcasted_iota(jnp.int32, (blocks_i, LANES), 0) * LANES + my_src * SRC_DEV
    sin_out, cos_out = sine_cosine(
        wrap(outer * generator, modulus).astype(f32) / modulus + shift
    )
    half = LANES // 2
    for block in range(blocks_i):
        rows = pl.ds(block * LANES, LANES)
        points = (
            sin_out[block : block + 1, :] * cos_in + cos_out[block : block + 1, :] * sin_in
        )
        high = points.astype(bf16)
        a_left[rows, :LANES] = high
        a_static[rows, :] = jnp.where(first, points - high.astype(f32), 0.0).astype(bf16)
    sin_in, cos_in = sin_in.T[:half, :], cos_in.T[:half, :]
    outside = jnp.concatenate(
        [sin_out, cos_out, jnp.zeros((LANES - 2 * blocks_i, LANES), f32)], 0
    ).T[:half, :]
    for block in range(blocks_i):
        cut = pl.ds(block * LANES, LANES)
        points = (
            outside[:, block : block + 1] * cos_in
            + outside[:, blocks_i + block : blocks_i + block + 1] * sin_in
        )
        near_ref[block : block + 1, :] = 0.5 * jnp.sum(points * points, 0, keepdims=True)
        high = points.astype(bf16)
        a_right[:half, cut] = high
        a_right[half : 2 * half, cut] = high
        a_right[2 * half : 3 * half, cut] = (points - high.astype(f32)).astype(bf16)
    a_right[3 * half :, :] = jnp.ones((half, SRC_DEV), bf16)

    for block in range(blocks_j):
        rows = pl.ds(block * LANES, LANES)
        part = targets_ref[:, block * LANES : (block + 1) * LANES]
        far_ref[block : block + 1, :] = 0.5 * jnp.sum(part * part, 0, keepdims=True)
        part = part * f32(scale)
        high = part.astype(bf16)
        low = part - high.astype(f32)
        turned = jnp.concatenate([high.astype(f32), low], 0).T
        b_left[rows, :LANES] = turned.astype(bf16)
        b_static[rows, :] = jnp.where(first, turned, 0.0).astype(bf16)
        b_right[:half, rows] = high
        b_right[half : 2 * half, rows] = low.astype(bf16)
        b_right[2 * half : 3 * half, rows] = high
    b_right[3 * half :, :] = jnp.ones((half, columns), bf16)

    weights = weights_ref[...] * f32(log2_e)
    far = far_ref[...] * f32(scale)
    log_count = f32(math.log2(modulus))
    potential_g = -far
    buffers = (buffer_0, buffer_1)
    share = blocks_i // HALVES
    for step in range(ITERS):
        place(weights + potential_g, b_static, b_left)

        def send(chunk, step=step):
            half, rest = divmod((chunk + 1) * WIDE, share * LANES)
            if rest:
                return
            half = half - 1
            cut = pl.ds(half * share, share)
            row_out[step, half] = row_tops[cut, :] + jnp.log(row_totals[cut, :]) * f32(log2_e)
            if step == 0 and half == 0:
                pl.semaphore_wait(barrier, src - 1 + tgt - 1)
            for number in range(tgt - 1):
                row_copy(step, half, number).start()

        sweep(b_left, a_right, buffers, (0, columns), row_tops, row_totals, send)
        if step == 0:
            peak = jnp.max(weights, keepdims=True)
            total = jnp.sum(jnp.exp2(weights - peak), keepdims=True)
            norm_out[...] = jnp.broadcast_to(
                peak + jnp.log(total) * f32(log2_e), (8, LANES)
            )
            for number in range(tgt - 1):
                norm_copy(number).start()
        parts, potential_f = [], []
        for half in range(HALVES):
            for number in range(tgt - 1):
                row_copy(step, half, number).wait_recv()
            potential_f.append(-log_sum(
                [row_out[step, half]]
                + [row_in[step, half, number] for number in range(tgt - 1)]
            ))
            rows = (half * share * LANES, share * LANES)
            place(potential_f[half], a_static, a_left, rows[0])
            sweep(a_left, b_right, buffers, rows, col_tops, col_totals)
            parts.append(col_tops[...] + jnp.log(col_totals[...]) * f32(log2_e))
        col_out[step] = log_sum(parts)
        for number in range(src - 1):
            col_copy(step, number).start()
        if step == 0:
            for number in range(tgt - 1):
                norm_copy(number).wait_recv()
            norm = log_sum(
                [norm_out[...]] + [norm_in[number] for number in range(tgt - 1)]
            )[0:1, :]
        for half in range(HALVES):
            for number in range(tgt - 1):
                row_copy(step, half, number).wait_send()
        if step == 0:
            for number in range(tgt - 1):
                norm_copy(number).wait_send()
        if step == ITERS - 1:
            for half in range(HALVES):
                cut = pl.ds(half * share, share)
                out_ref[cut, :] = (
                    (potential_f[half] + norm) * f32(1.0 / scale) + near_ref[cut, :]
                )
        for number in range(src - 1):
            col_copy(step, number).wait()
        sums = log_sum([col_out[step]] + [col_in[step, number] for number in range(src - 1)])
        potential_g = log_count - sums - norm
    out_ref[blocks_i:, :] = potential_g * f32(1.0 / scale) + far_ref[...]


def local(sizes, generator, shift, targets, log_weights):
    src, tgt = sizes
    columns = targets.shape[1]
    blocks_i, blocks_j = SRC_DEV // LANES, columns // LANES
    vmem = pl.BlockSpec(memory_space=pltpu.VMEM)
    dma = pltpu.SemaphoreType.DMA
    both = pl.pallas_call(
        functools.partial(kernel, sizes),
        out_shape=jax.ShapeDtypeStruct((blocks_i + blocks_j, LANES), f32),
        in_specs=[vmem] * 4,
        out_specs=vmem,
        scratch_shapes=[
            pltpu.VMEM((SRC_DEV, 2 * LANES), bf16),
            pltpu.VMEM((2 * LANES, SRC_DEV), bf16),
            pltpu.VMEM((SRC_DEV, LANES), bf16),
            pltpu.VMEM((columns, 2 * LANES), bf16),
            pltpu.VMEM((2 * LANES, columns), bf16),
            pltpu.VMEM((columns, LANES), bf16),
            pltpu.VMEM((max(SRC_DEV, columns), WIDE), f32),
            pltpu.VMEM((max(SRC_DEV, columns), WIDE), f32),
            pltpu.VMEM((8, LANES), f32),
            pltpu.VMEM((blocks_j, LANES), f32),
            pltpu.VMEM((blocks_i, LANES), f32),
            pltpu.VMEM((blocks_i, LANES), f32),
            pltpu.VMEM((blocks_i, LANES), f32),
            pltpu.VMEM((blocks_j, LANES), f32),
            pltpu.VMEM((blocks_j, LANES), f32),
            pltpu.VMEM((ITERS, HALVES, blocks_i // HALVES, LANES), f32),
            pltpu.VMEM((ITERS, HALVES, tgt - 1, blocks_i // HALVES, LANES), f32),
            pltpu.VMEM((ITERS, blocks_j, LANES), f32),
            pltpu.VMEM((ITERS, src - 1, blocks_j, LANES), f32),
            pltpu.VMEM((8, LANES), f32),
            pltpu.VMEM((tgt - 1, 8, LANES), f32),
            dma((ITERS, HALVES, tgt - 1)),
            dma((ITERS, HALVES, tgt - 1)),
            dma((ITERS, src - 1)),
            dma((ITERS, src - 1)),
            dma((tgt - 1,)),
            dma((tgt - 1,)),
        ],
        compiler_params=pltpu.CompilerParams(
            collective_id=0, has_side_effects=True, vmem_limit_bytes=LIMIT
        ),
    )(
        generator.reshape(1, -1),
        shift.reshape(1, -1),
        targets,
        log_weights.reshape(blocks_j, LANES),
    )
    return both[:blocks_i].reshape(-1), both[blocks_i:].reshape(-1)


def solution(mesh):
    sizes = (mesh.shape["src"], mesh.shape["tgt"])
    in_specs = (P(), P(), P(None, "tgt"), P("tgt"))
    out_specs = (P("src"), P("tgt"))
    return jax.shard_map(
        functools.partial(local, sizes), mesh=mesh,
        in_specs=in_specs, out_specs=out_specs, check_vma=False,
    )
```

```python
import functools
import math

import jax
import jax.numpy as jnp
from jax import lax
from jax.experimental import pallas as pl
from jax.experimental.pallas import tpu as pltpu
from jax.sharding import PartitionSpec as P

SRC_DEV = 2048
ITERS = 2
LANES = 128
WIDE = 256
TILE = 64
LIMIT = 40 * 2**20
HALVES = 2

blur_level = 0.1
log2_e = math.log2(math.e)
scale = log2_e / blur_level
MESH = pl.DeviceIdType.MESH
f32 = jnp.float32
bf16 = jnp.bfloat16


def sine_cosine(turns):
    half = (turns - jnp.round(turns)) * f32(math.pi)
    square = half * half
    sine = f32(1.0 / math.factorial(13))
    cosine = f32(1.0 / math.factorial(12))
    for order in (11, 9, 7, 5, 3, 1):
        sign = -1.0 if (order // 2) % 2 else 1.0
        sine = sine * square + f32(sign / math.factorial(order))
    for order in (10, 8, 6, 4, 2, 0):
        sign = -1.0 if (order // 2) % 2 else 1.0
        cosine = cosine * square + f32(sign / math.factorial(order))
    sine = sine * half
    return 2.0 * sine * cosine, 1.0 - 2.0 * sine * sine


def wrap(value, modulus):
    return value & (modulus - 1) if modulus & (modulus - 1) == 0 else lax.rem(value, modulus)


def log_sum(terms):
    top = functools.reduce(jnp.maximum, terms)
    total = functools.reduce(jnp.add, [jnp.exp2(term - top) for term in terms])
    return top + jnp.log(total) * f32(log2_e)


def fold(combine, scores, rows):
    running = None
    for start in range(0, rows, TILE):
        running = combine(running, scores[pl.ds(start, TILE), :])
    return running


def sweep(left_ref, right_ref, buffers, rows, tops, totals, after=None):
    first, size = rows
    count = right_ref.shape[1] // WIDE

    def product(chunk):
        scores = jnp.dot(
            left_ref[pl.ds(first, size), :],
            right_ref[:, pl.ds(chunk * WIDE, WIDE)],
            preferred_element_type=f32,
        )
        buffers[chunk % 2][pl.ds(0, size), :] = scores
        running = scores[:TILE]
        for start in range(TILE, size, TILE):
            running = jnp.maximum(running, scores[start : start + TILE])
        return jnp.max(running, 0, keepdims=True)

    later = product(0)
    for chunk in range(count):
        top = later
        if chunk + 1 < count:
            later = product(chunk + 1)
        scores = buffers[chunk % 2]
        shift = jnp.broadcast_to(top, (TILE, WIDE))

        def add(total, part):
            part = jnp.exp2(part - shift)
            return part if total is None else total + part

        total = jnp.sum(fold(add, scores, size), 0, keepdims=True)
        for piece in range(WIDE // LANES):
            at = chunk * (WIDE // LANES) + piece
            cut = slice(piece * LANES, (piece + 1) * LANES)
            tops[at : at + 1, :] = top[:, cut]
            totals[at : at + 1, :] = total[:, cut]
        if after is not None:
            after(chunk)


def place(values, static, left_ref, first=0):
    blocks = values.shape[0]
    high = values.astype(bf16).astype(f32)
    rest = values - high
    mid = rest.astype(bf16).astype(f32)
    low = rest - mid
    filler = [jnp.zeros((LANES // 2, LANES), f32), high, mid, low]
    spare = LANES // 2 - 3 * blocks
    if spare:
        filler.append(jnp.zeros((spare, LANES), f32))
    turned = jnp.concatenate(filler, 0).T.astype(bf16)
    lane = lax.broadcasted_iota(jnp.int32, (16, LANES), 1)
    owner = jnp.where(lane < LANES // 2, -1, wrap(lane, blocks))
    for block in range(blocks):
        rows = pl.ds(first + block * LANES, LANES)
        chosen = jnp.where(owner == block, 1.0, 0.0).astype(bf16)
        chosen = jnp.concatenate([chosen] * (LANES // 16), 0)
        left_ref[rows, LANES:] = static[rows, :] + turned * chosen


def kernel(
    sizes, generator_ref, shift_ref, targets_ref, weights_ref, out_ref,
    a_left, a_right, a_static, b_left, b_right, b_static, buffer_0, buffer_1, pair, far_ref, near_ref,
    row_tops, row_totals, col_tops, col_totals,
    row_out, row_in, col_out, col_in, norm_out, norm_in,
    row_send, row_recv, col_send, col_recv, norm_send, norm_recv,
):
    src, tgt = sizes
    modulus = SRC_DEV * src
    my_src, my_tgt = lax.axis_index("src"), lax.axis_index("tgt")
    src_peers = [lax.rem(my_src + step, src) for step in range(1, src)]
    tgt_peers = [lax.rem(my_tgt + step, tgt) for step in range(1, tgt)]
    barrier = pltpu.get_barrier_semaphore()
    for peer in tgt_peers:
        pl.semaphore_signal(barrier, inc=1, device_id=(my_src, peer), device_id_type=MESH)
    for peer in src_peers:
        pl.semaphore_signal(barrier, inc=1, device_id=(peer, my_tgt), device_id_type=MESH)

    def row_copy(step, half, number):
        return pltpu.make_async_remote_copy(
            src_ref=row_out.at[step, half], dst_ref=row_in.at[step, half, number],
            send_sem=row_send.at[step, half, number],
            recv_sem=row_recv.at[step, half, number],
            device_id=(my_src, tgt_peers[number]), device_id_type=MESH,
        )

    def col_copy(step, number):
        return pltpu.make_async_remote_copy(
            src_ref=col_out.at[step], dst_ref=col_in.at[step, number],
            send_sem=col_send.at[step, number], recv_sem=col_recv.at[step, number],
            device_id=(src_peers[number], my_tgt), device_id_type=MESH,
        )

    def norm_copy(number):
        return pltpu.make_async_remote_copy(
            src_ref=norm_out, dst_ref=norm_in.at[number],
            send_sem=norm_send.at[number], recv_sem=norm_recv.at[number],
            device_id=(my_src, tgt_peers[number]), device_id_type=MESH,
        )

    blocks_i = SRC_DEV // LANES
    columns = targets_ref.shape[1]
    blocks_j = columns // LANES
    lane = lax.broadcasted_iota(jnp.int32, (LANES, LANES), 1)
    first = lane < LANES // 2

    pair[0:1, : LANES // 2] = generator_ref[...].astype(f32)
    pair[1:2, : LANES // 2] = shift_ref[...]
    both = pair[0:2, :]
    low_half = lax.broadcasted_iota(jnp.int32, (2, LANES), 1) < LANES // 2
    both = jnp.where(low_half, both, pltpu.roll(both, LANES // 2, 1))
    generator = both[0:1, :].astype(jnp.int32)
    shift = both[1:2, :]
    inner = lax.broadcasted_iota(jnp.int32, (LANES, LANES), 0)
    sin_in, cos_in = sine_cosine(
        wrap(inner * generator, modulus).astype(f32) / modulus
    )
    outer = lax.broadcasted_iota(jnp.int32, (blocks_i, LANES), 0) * LANES + my_src * SRC_DEV
    sin_out, cos_out = sine_cosine(
        wrap(outer * generator, modulus).astype(f32) / modulus + shift
    )
    half = LANES // 2
    sin_turned, cos_turned = sin_in.T[:half, :], cos_in.T[:half, :]
    outside = jnp.concatenate(
        [sin_out, cos_out, jnp.zeros((LANES - 2 * blocks_i, LANES), f32)], 0
    ).T[:half, :]
    for block in range(blocks_i):
        cut = pl.ds(block * LANES, LANES)
        points = (
            outside[:, block : block + 1] * cos_turned
            + outside[:, blocks_i + block : blocks_i + block + 1] * sin_turned
        )
        near_ref[block : block + 1, :] = 0.5 * jnp.sum(points * points, 0, keepdims=True)
        high = points.astype(bf16)
        a_right[:half, cut] = high
        a_right[half : 2 * half, cut] = high
        a_right[2 * half : 3 * half, cut] = (points - high.astype(f32)).astype(bf16)
    a_right[3 * half :, :] = jnp.ones((half, SRC_DEV), bf16)

    for block in range(blocks_j):
        rows = pl.ds(block * LANES, LANES)
        part = targets_ref[:, block * LANES : (block + 1) * LANES]
        far_ref[block : block + 1, :] = 0.5 * jnp.sum(part * part, 0, keepdims=True)
        part = part * f32(scale)
        high = part.astype(bf16)
        low = part - high.astype(f32)
        turned = jnp.concatenate([high.astype(f32), low], 0).T
        b_left[rows, :LANES] = turned.astype(bf16)
        b_static[rows, :] = jnp.where(first, turned, 0.0).astype(bf16)

    def prepare():
        for block in range(blocks_i):
            rows = pl.ds(block * LANES, LANES)
            points = (
                sin_out[block : block + 1, :] * cos_in
                + cos_out[block : block + 1, :] * sin_in
            )
            high = points.astype(bf16)
            a_left[rows, :LANES] = high
            a_static[rows, :] = jnp.where(first, points - high.astype(f32), 0.0).astype(bf16)
        for block in range(blocks_j):
            cut = pl.ds(block * LANES, LANES)
            part = targets_ref[:, block * LANES : (block + 1) * LANES] * f32(scale)
            high = part.astype(bf16)
            b_right[:half, cut] = high
            b_right[half : 2 * half, cut] = (part - high.astype(f32)).astype(bf16)
            b_right[2 * half : 3 * half, cut] = high
        b_right[3 * half :, :] = jnp.ones((half, columns), bf16)

    weights = weights_ref[...] * f32(log2_e)
    far = far_ref[...] * f32(scale)
    log_count = f32(math.log2(modulus))
    potential_g = -far
    buffers = (buffer_0, buffer_1)
    share = blocks_i // HALVES
    for step in range(ITERS):
        place(weights + potential_g, b_static, b_left)

        def send(chunk, step=step):
            half, rest = divmod((chunk + 1) * WIDE, share * LANES)
            if rest:
                return
            half = half - 1
            cut = pl.ds(half * share, share)
            row_out[step, half] = row_tops[cut, :] + jnp.log(row_totals[cut, :]) * f32(log2_e)
            if step == 0 and half == 0:
                pl.semaphore_wait(barrier, src - 1 + tgt - 1)
            for number in range(tgt - 1):
                row_copy(step, half, number).start()

        sweep(b_left, a_right, buffers, (0, columns), row_tops, row_totals, send)
        if step == 0:
            peak = jnp.max(weights, keepdims=True)
            total = jnp.sum(jnp.exp2(weights - peak), keepdims=True)
            norm_out[...] = jnp.broadcast_to(
                peak + jnp.log(total) * f32(log2_e), (8, LANES)
            )
            for number in range(tgt - 1):
                norm_copy(number).start()
            prepare()
        parts, potential_f = [], []
        for half in range(HALVES):
            for number in range(tgt - 1):
                row_copy(step, half, number).wait_recv()
            potential_f.append(-log_sum(
                [row_out[step, half]]
                + [row_in[step, half, number] for number in range(tgt - 1)]
            ))
            rows = (half * share * LANES, share * LANES)
            place(potential_f[half], a_static, a_left, rows[0])
            sweep(a_left, b_right, buffers, rows, col_tops, col_totals)
            parts.append(col_tops[...] + jnp.log(col_totals[...]) * f32(log2_e))
        col_out[step] = log_sum(parts)
        for number in range(src - 1):
            col_copy(step, number).start()
        if step == 0:
            for number in range(tgt - 1):
                norm_copy(number).wait_recv()
            norm = log_sum(
                [norm_out[...]] + [norm_in[number] for number in range(tgt - 1)]
            )[0:1, :]
        for half in range(HALVES):
            for number in range(tgt - 1):
                row_copy(step, half, number).wait_send()
        if step == 0:
            for number in range(tgt - 1):
                norm_copy(number).wait_send()
        if step == ITERS - 1:
            for half in range(HALVES):
                cut = pl.ds(half * share, share)
                out_ref[cut, :] = (
                    (potential_f[half] + norm) * f32(1.0 / scale) + near_ref[cut, :]
                )
        for number in range(src - 1):
            col_copy(step, number).wait()
        sums = log_sum([col_out[step]] + [col_in[step, number] for number in range(src - 1)])
        potential_g = log_count - sums - norm
    out_ref[blocks_i:, :] = potential_g * f32(1.0 / scale) + far_ref[...]


def local(sizes, generator, shift, targets, log_weights):
    src, tgt = sizes
    columns = targets.shape[1]
    blocks_i, blocks_j = SRC_DEV // LANES, columns // LANES
    vmem = pl.BlockSpec(memory_space=pltpu.VMEM)
    dma = pltpu.SemaphoreType.DMA
    both = pl.pallas_call(
        functools.partial(kernel, sizes),
        out_shape=jax.ShapeDtypeStruct((blocks_i + blocks_j, LANES), f32),
        in_specs=[vmem] * 4,
        out_specs=vmem,
        scratch_shapes=[
            pltpu.VMEM((SRC_DEV, 2 * LANES), bf16),
            pltpu.VMEM((2 * LANES, SRC_DEV), bf16),
            pltpu.VMEM((SRC_DEV, LANES), bf16),
            pltpu.VMEM((columns, 2 * LANES), bf16),
            pltpu.VMEM((2 * LANES, columns), bf16),
            pltpu.VMEM((columns, LANES), bf16),
            pltpu.VMEM((max(SRC_DEV, columns), WIDE), f32),
            pltpu.VMEM((max(SRC_DEV, columns), WIDE), f32),
            pltpu.VMEM((8, LANES), f32),
            pltpu.VMEM((blocks_j, LANES), f32),
            pltpu.VMEM((blocks_i, LANES), f32),
            pltpu.VMEM((blocks_i, LANES), f32),
            pltpu.VMEM((blocks_i, LANES), f32),
            pltpu.VMEM((blocks_j, LANES), f32),
            pltpu.VMEM((blocks_j, LANES), f32),
            pltpu.VMEM((ITERS, HALVES, blocks_i // HALVES, LANES), f32),
            pltpu.VMEM((ITERS, HALVES, tgt - 1, blocks_i // HALVES, LANES), f32),
            pltpu.VMEM((ITERS, blocks_j, LANES), f32),
            pltpu.VMEM((ITERS, src - 1, blocks_j, LANES), f32),
            pltpu.VMEM((8, LANES), f32),
            pltpu.VMEM((tgt - 1, 8, LANES), f32),
            dma((ITERS, HALVES, tgt - 1)),
            dma((ITERS, HALVES, tgt - 1)),
            dma((ITERS, src - 1)),
            dma((ITERS, src - 1)),
            dma((tgt - 1,)),
            dma((tgt - 1,)),
        ],
        compiler_params=pltpu.CompilerParams(
            collective_id=0, has_side_effects=True, vmem_limit_bytes=LIMIT
        ),
    )(
        generator.reshape(1, -1),
        shift.reshape(1, -1),
        targets,
        log_weights.reshape(blocks_j, LANES),
    )
    return both[:blocks_i].reshape(-1), both[blocks_i:].reshape(-1)


def solution(mesh):
    sizes = (mesh.shape["src"], mesh.shape["tgt"])
    in_specs = (P(), P(), P(None, "tgt"), P("tgt"))
    out_specs = (P("src"), P("tgt"))
    return jax.shard_map(
        functools.partial(local, sizes), mesh=mesh,
        in_specs=in_specs, out_specs=out_specs, check_vma=False,
    )
```

```python
import functools
import math

import jax
import jax.numpy as jnp
from jax import lax
from jax.experimental import pallas as pl
from jax.experimental.pallas import tpu as pltpu
from jax.sharding import PartitionSpec as P

SRC_DEV = 2048
ITERS = 2
LANES = 128
WIDE = 256
TILE = 64
LIMIT = 54 * 2**20 - 2**17
HALVES = 2

blur_level = 0.1
log2_e = math.log2(math.e)
scale = log2_e / blur_level
MESH = pl.DeviceIdType.MESH
f32 = jnp.float32
bf16 = jnp.bfloat16


def sine_cosine(turns):
    half = (turns - jnp.round(turns)) * f32(math.pi)
    square = half * half
    sine = f32(1.0 / math.factorial(13))
    cosine = f32(1.0 / math.factorial(12))
    for order in (11, 9, 7, 5, 3, 1):
        sign = -1.0 if (order // 2) % 2 else 1.0
        sine = sine * square + f32(sign / math.factorial(order))
    for order in (10, 8, 6, 4, 2, 0):
        sign = -1.0 if (order // 2) % 2 else 1.0
        cosine = cosine * square + f32(sign / math.factorial(order))
    sine = sine * half
    return 2.0 * sine * cosine, 1.0 - 2.0 * sine * sine


def wrap(value, modulus):
    return value & (modulus - 1) if modulus & (modulus - 1) == 0 else lax.rem(value, modulus)


def log_sum(terms):
    top = functools.reduce(jnp.maximum, terms)
    total = functools.reduce(jnp.add, [jnp.exp2(term - top) for term in terms])
    return top + jnp.log(total) * f32(log2_e)


def fold(combine, scores, rows):
    running = None
    for start in range(0, rows, TILE):
        running = combine(running, scores[pl.ds(start, TILE), :])
    return running


def sweep(left_ref, right_ref, buffers, rows, tops, totals, after=None):
    first, size = rows
    count = right_ref.shape[1] // WIDE

    def product(chunk):
        scores = jnp.dot(
            left_ref[pl.ds(first, size), :],
            right_ref[:, pl.ds(chunk * WIDE, WIDE)],
            preferred_element_type=f32,
        )
        buffers[chunk % 2][pl.ds(0, size), :] = scores
        running = scores[:TILE]
        for start in range(TILE, size, TILE):
            running = jnp.maximum(running, scores[start : start + TILE])
        return jnp.max(running, 0, keepdims=True)

    later = product(0)
    for chunk in range(count):
        top = later
        if chunk + 1 < count:
            later = product(chunk + 1)
        scores = buffers[chunk % 2]
        shift = jnp.broadcast_to(top, (TILE, WIDE))

        def add(total, part):
            part = jnp.exp2(part - shift)
            return part if total is None else total + part

        total = jnp.sum(fold(add, scores, size), 0, keepdims=True)
        for piece in range(WIDE // LANES):
            at = chunk * (WIDE // LANES) + piece
            cut = slice(piece * LANES, (piece + 1) * LANES)
            tops[at : at + 1, :] = top[:, cut]
            totals[at : at + 1, :] = total[:, cut]
        if after is not None:
            after(chunk)


def place(values, static, left_ref, first=0):
    blocks = values.shape[0]
    high = values.astype(bf16).astype(f32)
    rest = values - high
    mid = rest.astype(bf16).astype(f32)
    low = rest - mid
    filler = [jnp.zeros((LANES // 2, LANES), f32), high, mid, low]
    spare = LANES // 2 - 3 * blocks
    if spare:
        filler.append(jnp.zeros((spare, LANES), f32))
    turned = jnp.concatenate(filler, 0).T.astype(bf16)
    lane = lax.broadcasted_iota(jnp.int32, (16, LANES), 1)
    owner = jnp.where(lane < LANES // 2, -1, wrap(lane, blocks))
    for block in range(blocks):
        rows = pl.ds(first + block * LANES, LANES)
        chosen = jnp.where(owner == block, 1.0, 0.0).astype(bf16)
        chosen = jnp.concatenate([chosen] * (LANES // 16), 0)
        left_ref[rows, LANES:] = static[rows, :] + turned * chosen


def kernel(
    sizes, generator_ref, shift_ref, targets_hbm, weights_ref, out_ref, targets_ref,
    a_left, a_right, a_static, b_left, b_right, b_static, buffer_0, buffer_1, pair, far_ref, near_ref,
    row_tops, row_totals, col_tops, col_totals,
    row_out, row_in, col_out, col_in, norm_out, norm_in,
    row_send, row_recv, col_send, col_recv, norm_send, norm_recv, load,
):
    src, tgt = sizes
    modulus = SRC_DEV * src
    my_src, my_tgt = lax.axis_index("src"), lax.axis_index("tgt")
    src_peers = [lax.rem(my_src + step, src) for step in range(1, src)]
    tgt_peers = [lax.rem(my_tgt + step, tgt) for step in range(1, tgt)]
    fetch = pltpu.make_async_copy(targets_hbm, targets_ref, load)
    fetch.start()
    barrier = pltpu.get_barrier_semaphore()
    for peer in tgt_peers:
        pl.semaphore_signal(barrier, inc=1, device_id=(my_src, peer), device_id_type=MESH)
    for peer in src_peers:
        pl.semaphore_signal(barrier, inc=1, device_id=(peer, my_tgt), device_id_type=MESH)

    def row_copy(step, half, number):
        return pltpu.make_async_remote_copy(
            src_ref=row_out.at[step, half], dst_ref=row_in.at[step, half, number],
            send_sem=row_send.at[step, half, number],
            recv_sem=row_recv.at[step, half, number],
            device_id=(my_src, tgt_peers[number]), device_id_type=MESH,
        )

    def col_copy(step, number):
        return pltpu.make_async_remote_copy(
            src_ref=col_out.at[step], dst_ref=col_in.at[step, number],
            send_sem=col_send.at[step, number], recv_sem=col_recv.at[step, number],
            device_id=(src_peers[number], my_tgt), device_id_type=MESH,
        )

    def norm_copy(number):
        return pltpu.make_async_remote_copy(
            src_ref=norm_out, dst_ref=norm_in.at[number],
            send_sem=norm_send.at[number], recv_sem=norm_recv.at[number],
            device_id=(my_src, tgt_peers[number]), device_id_type=MESH,
        )

    blocks_i = SRC_DEV // LANES
    columns = targets_ref.shape[1]
    blocks_j = columns // LANES
    lane = lax.broadcasted_iota(jnp.int32, (LANES, LANES), 1)
    first = lane < LANES // 2

    pair[0:1, : LANES // 2] = generator_ref[...].astype(f32)
    pair[1:2, : LANES // 2] = shift_ref[...]
    both = pair[0:2, :]
    low_half = lax.broadcasted_iota(jnp.int32, (2, LANES), 1) < LANES // 2
    both = jnp.where(low_half, both, pltpu.roll(both, LANES // 2, 1))
    generator = both[0:1, :].astype(jnp.int32)
    shift = both[1:2, :]
    inner = lax.broadcasted_iota(jnp.int32, (LANES, LANES), 0)
    sin_in, cos_in = sine_cosine(
        wrap(inner * generator, modulus).astype(f32) / modulus
    )
    outer = lax.broadcasted_iota(jnp.int32, (blocks_i, LANES), 0) * LANES + my_src * SRC_DEV
    sin_out, cos_out = sine_cosine(
        wrap(outer * generator, modulus).astype(f32) / modulus + shift
    )
    half = LANES // 2
    sin_turned, cos_turned = sin_in.T[:half, :], cos_in.T[:half, :]
    outside = jnp.concatenate(
        [sin_out, cos_out, jnp.zeros((LANES - 2 * blocks_i, LANES), f32)], 0
    ).T[:half, :]
    for block in range(blocks_i):
        cut = pl.ds(block * LANES, LANES)
        points = (
            outside[:, block : block + 1] * cos_turned
            + outside[:, blocks_i + block : blocks_i + block + 1] * sin_turned
        )
        near_ref[block : block + 1, :] = 0.5 * jnp.sum(points * points, 0, keepdims=True)
        high = points.astype(bf16)
        a_right[:half, cut] = high
        a_right[half : 2 * half, cut] = high
        a_right[2 * half : 3 * half, cut] = (points - high.astype(f32)).astype(bf16)
    a_right[3 * half :, :] = jnp.ones((half, SRC_DEV), bf16)

    fetch.wait()
    for block in range(blocks_j):
        rows = pl.ds(block * LANES, LANES)
        part = targets_ref[:, block * LANES : (block + 1) * LANES]
        far_ref[block : block + 1, :] = 0.5 * jnp.sum(part * part, 0, keepdims=True)
        part = part * f32(scale)
        high = part.astype(bf16)
        low = part - high.astype(f32)
        turned = jnp.concatenate([high.astype(f32), low], 0).T
        b_left[rows, :LANES] = turned.astype(bf16)
        b_static[rows, :] = jnp.where(first, turned, 0.0).astype(bf16)

    def prepare():
        for block in range(blocks_i):
            rows = pl.ds(block * LANES, LANES)
            points = (
                sin_out[block : block + 1, :] * cos_in
                + cos_out[block : block + 1, :] * sin_in
            )
            high = points.astype(bf16)
            a_left[rows, :LANES] = high
            a_static[rows, :] = jnp.where(first, points - high.astype(f32), 0.0).astype(bf16)
        for block in range(blocks_j):
            cut = pl.ds(block * LANES, LANES)
            part = targets_ref[:, block * LANES : (block + 1) * LANES] * f32(scale)
            high = part.astype(bf16)
            b_right[:half, cut] = high
            b_right[half : 2 * half, cut] = (part - high.astype(f32)).astype(bf16)
            b_right[2 * half : 3 * half, cut] = high
        b_right[3 * half :, :] = jnp.ones((half, columns), bf16)

    weights = weights_ref[...] * f32(log2_e)
    far = far_ref[...] * f32(scale)
    log_count = f32(math.log2(modulus))
    potential_g = -far
    buffers = (buffer_0, buffer_1)
    share = blocks_i // HALVES
    for step in range(ITERS):
        place(weights + potential_g, b_static, b_left)

        def send(chunk, step=step):
            half, rest = divmod((chunk + 1) * WIDE, share * LANES)
            if rest:
                return
            half = half - 1
            cut = pl.ds(half * share, share)
            row_out[step, half] = row_tops[cut, :] + jnp.log(row_totals[cut, :]) * f32(log2_e)
            if step == 0 and half == 0:
                pl.semaphore_wait(barrier, src - 1 + tgt - 1)
            for number in range(tgt - 1):
                row_copy(step, half, number).start()

        sweep(b_left, a_right, buffers, (0, columns), row_tops, row_totals, send)
        if step == 0:
            peak = jnp.max(weights, keepdims=True)
            total = jnp.sum(jnp.exp2(weights - peak), keepdims=True)
            norm_out[...] = jnp.broadcast_to(
                peak + jnp.log(total) * f32(log2_e), (8, LANES)
            )
            for number in range(tgt - 1):
                norm_copy(number).start()
            prepare()
        parts, potential_f = [], []
        for half in range(HALVES):
            for number in range(tgt - 1):
                row_copy(step, half, number).wait_recv()
            potential_f.append(-log_sum(
                [row_out[step, half]]
                + [row_in[step, half, number] for number in range(tgt - 1)]
            ))
            rows = (half * share * LANES, share * LANES)
            place(potential_f[half], a_static, a_left, rows[0])
            sweep(a_left, b_right, buffers, rows, col_tops, col_totals)
            parts.append(col_tops[...] + jnp.log(col_totals[...]) * f32(log2_e))
        col_out[step] = log_sum(parts)
        for number in range(src - 1):
            col_copy(step, number).start()
        if step == 0:
            for number in range(tgt - 1):
                norm_copy(number).wait_recv()
            norm = log_sum(
                [norm_out[...]] + [norm_in[number] for number in range(tgt - 1)]
            )[0:1, :]
        for half in range(HALVES):
            for number in range(tgt - 1):
                row_copy(step, half, number).wait_send()
        if step == 0:
            for number in range(tgt - 1):
                norm_copy(number).wait_send()
        if step == ITERS - 1:
            for half in range(HALVES):
                cut = pl.ds(half * share, share)
                out_ref[cut, :] = (
                    (potential_f[half] + norm) * f32(1.0 / scale) + near_ref[cut, :]
                )
        for number in range(src - 1):
            col_copy(step, number).wait()
        sums = log_sum([col_out[step]] + [col_in[step, number] for number in range(src - 1)])
        potential_g = log_count - sums - norm
    out_ref[blocks_i:, :] = potential_g * f32(1.0 / scale) + far_ref[...]


def local(sizes, generator, shift, targets, log_weights):
    src, tgt = sizes
    columns = targets.shape[1]
    blocks_i, blocks_j = SRC_DEV // LANES, columns // LANES
    vmem = pl.BlockSpec(memory_space=pltpu.VMEM)
    dma = pltpu.SemaphoreType.DMA
    both = pl.pallas_call(
        functools.partial(kernel, sizes),
        out_shape=jax.ShapeDtypeStruct((blocks_i + blocks_j, LANES), f32),
        in_specs=[vmem, vmem, pl.BlockSpec(memory_space=pltpu.HBM), vmem],
        out_specs=vmem,
        scratch_shapes=[
            pltpu.VMEM(targets.shape, f32),
            pltpu.VMEM((SRC_DEV, 2 * LANES), bf16),
            pltpu.VMEM((2 * LANES, SRC_DEV), bf16),
            pltpu.VMEM((SRC_DEV, LANES), bf16),
            pltpu.VMEM((columns, 2 * LANES), bf16),
            pltpu.VMEM((2 * LANES, columns), bf16),
            pltpu.VMEM((columns, LANES), bf16),
            pltpu.VMEM((max(SRC_DEV, columns), WIDE), f32),
            pltpu.VMEM((max(SRC_DEV, columns), WIDE), f32),
            pltpu.VMEM((8, LANES), f32),
            pltpu.VMEM((blocks_j, LANES), f32),
            pltpu.VMEM((blocks_i, LANES), f32),
            pltpu.VMEM((blocks_i, LANES), f32),
            pltpu.VMEM((blocks_i, LANES), f32),
            pltpu.VMEM((blocks_j, LANES), f32),
            pltpu.VMEM((blocks_j, LANES), f32),
            pltpu.VMEM((ITERS, HALVES, blocks_i // HALVES, LANES), f32),
            pltpu.VMEM((ITERS, HALVES, tgt - 1, blocks_i // HALVES, LANES), f32),
            pltpu.VMEM((ITERS, blocks_j, LANES), f32),
            pltpu.VMEM((ITERS, src - 1, blocks_j, LANES), f32),
            pltpu.VMEM((8, LANES), f32),
            pltpu.VMEM((tgt - 1, 8, LANES), f32),
            dma((ITERS, HALVES, tgt - 1)),
            dma((ITERS, HALVES, tgt - 1)),
            dma((ITERS, src - 1)),
            dma((ITERS, src - 1)),
            dma((tgt - 1,)),
            dma((tgt - 1,)),
            dma,
        ],
        compiler_params=pltpu.CompilerParams(
            collective_id=0, has_side_effects=True, vmem_limit_bytes=LIMIT
        ),
    )(
        generator.reshape(1, -1),
        shift.reshape(1, -1),
        targets,
        log_weights.reshape(blocks_j, LANES),
    )
    return both[:blocks_i].reshape(-1), both[blocks_i:].reshape(-1)


def solution(mesh):
    sizes = (mesh.shape["src"], mesh.shape["tgt"])
    in_specs = (P(), P(), P(None, "tgt"), P("tgt"))
    out_specs = (P("src"), P("tgt"))
    return jax.shard_map(
        functools.partial(local, sizes), mesh=mesh,
        in_specs=in_specs, out_specs=out_specs, check_vma=False,
    )
```
